32 devices in a mesh: expert: 16 (over z, y, x), tensor: 2 (over core).
Axes of the slice: x: 2, y: 2, z: 4, core: 2. Of those that a mesh axis runs over, the one named last changes fastest.
Arguments:
- tokens: bfloat16 [512, 4096], P('expert'), may hold values from -6 to 6
- routes: int32 [512, 8], P('expert'), may hold values from 0 to 15, all different within a row; in each aligned block of 32 rows (0 to 31, 32 to 63, ...) at most 24 rows name the same one
- route_weights: float32 [512, 8], P('expert'), may hold values from 0.1 to 1
- learner_weights: bfloat16 [16, 4096, 1536], P(None, 'expert', 'tensor'), may hold values from -5 to 5
Outputs:
- combined: bfloat16 [512, 1536], P('expert', 'tensor')
- expert_amax: float32 [16], P('expert')
The draws below stay inside these ranges and needn't reach their ends.
Inputs may be any that keep to these rules, and one draw needn't show every extreme that they name: `routes`: each row names 8 different experts; within the 32 rows of one index of expert no expert is named by more than 24 rows, a bound that some block reaches there.
All inputs are finite; a program needn't handle non-finite values.
Results may differ from the reference program's by a relative error of at most 0.0049.
Values may be sent and summed in bfloat16 or wider, within the bound.
No kernel may reach another device: no remote copies, remote signals or barrier semaphores. Data moves between devices by JAX's collectives and lax.ppermute only.
A program may use at most 64 MiB of HBM per device.

```python
import math
import jax
import jax.numpy as jnp
import numpy as np
from jax import lax

D = 4096
FF = 1536
TOP = 8
TOK_DEV = 32
EXPERTS = 16
CAP = 24
TOKENS = 512
N_EXPERT = 16


def draw_learner_weights(key, part):
    first_key, second_key, third_key = jax.random.split(key, 3)
    values = jnp.clip(jax.random.normal(first_key, (EXPERTS, D, FF), jnp.float32), -4.5, 4.5)
    row_scale = jnp.exp(jax.random.uniform(second_key, (EXPERTS, D, 1), jnp.float32, -1.15, 1.15))
    column_scale = jnp.exp(jax.random.uniform(third_key, (EXPERTS, 1, FF), jnp.float32, -1.7, 1.7))
    scaled = values * row_scale * column_scale / math.sqrt(2.15 * D)
    return scaled.astype(jnp.bfloat16)


def levels(stream_key, extent, shards, least, high):
    factor_of, own = 1.0, jax.random.fold_in(stream_key, 6)
    for position, parts in shards:
        draws = jnp.exp(jax.random.uniform(jax.random.fold_in(own, position), (parts,), jnp.float32, least / len(shards), high / len(shards)))
        factor_of = factor_of * jnp.repeat(draws, extent[position] // parts).reshape([-1 if axis == position else 1 for axis in range(len(extent))])
    return factor_of


def assign_block(rng, own, number, rows, number_of, top, most, slope):
    ranking = jax.random.permutation(rng, number_of)
    heavy_load, ordinary = load_shares(number_of, rows * top, most, slope, True), load_shares(number_of, rows * top, most, slope, False)
    places = jnp.arange(number_of)

    def named(sizes, offset_by):
        used = int((sizes > 0).sum())
        fixed = max(1, used // 4)
        passed = fixed + (places - fixed + offset_by * (used - fixed)) % max(1, number_of - fixed)
        return jnp.zeros((number_of,), jnp.int32).at[ranking[jnp.where(places < fixed, places, passed)]].set(jnp.asarray(sizes, jnp.int32))

    sizes = jnp.where(number % 4 == 0, named(heavy_load, number // 4), named(ordinary, number - number // 4 - 1))
    mixed = jax.random.permutation(jax.random.fold_in(own, 3), number_of)
    giver, taker = mixed[0:number_of // 2 * 2:2], mixed[1:number_of // 2 * 2:2]
    slack = jnp.minimum(sizes[giver] - 1, most - sizes[taker]) // 2
    slack = jnp.where((giver == ranking[0]) | (taker == ranking[0]) | (sizes[taker] == 0), 0, jnp.maximum(slack, 0))
    passed = jax.random.randint(jax.random.fold_in(own, 4), (number_of // 2,), 0, 1 << 20) % (slack + 1)
    sizes = sizes.at[giver].add(-passed).at[taker].add(passed)
    labels = jnp.searchsorted(jnp.cumsum(sizes), jnp.arange(rows * top), side="right").astype(jnp.int32)
    grid = labels.reshape(top, rows).T
    grid = grid[jax.random.permutation(jax.random.fold_in(own, 1), rows)]
    offset_by = jax.random.randint(jax.random.fold_in(own, 2), (rows, 1), 0, top)
    return jnp.take_along_axis(grid, (jnp.arange(top)[None, :] + offset_by) % top, axis=1)


def load_shares(count, total, reach, skew, full):
    weights = [(1 << 20) // math.isqrt(standing ** skew) + 1 for standing in range(1, count + 1)]
    largest = reach if full else min(reach, max(-(-total // count), total * weights[0] // sum(weights)))
    least = 1 if total - largest >= count - 1 else 0
    counts, spare = [largest] + [least] * (count - 1), total - largest - least * (count - 1)
    while spare > 0:
        movable = [i for i in range(1, count) if counts[i] < largest] or [i for i in range(1, count) if counts[i] < reach]
        pool, remaining = sum([weights[i] for i in movable]), spare
        for i in movable:
            more = min(reach - counts[i], max(1, remaining * weights[i] // pool), spare)
            counts[i] = counts[i] + more
            spare = spare - more
    return np.array(counts)


def scatter_about(stream_key, extent, deviation, most, shards=(), held_as=jnp.bfloat16):
    drawn = deviation * jax.random.normal(stream_key, extent, jnp.float32)
    if shards:
        drawn = drawn * levels(stream_key, extent, shards, -0.22, 0.18)
    return jnp.clip(drawn, -most, most).astype(held_as)


def setup_inputs(seed: int = 0) -> dict:
    keys = jax.random.split(jax.random.key(seed), 5)
    tokens = scatter_about(keys[0], (TOKENS, D), 1.0, 6.0, ((0, 16),))
    routes_keys = jax.random.split(jax.random.fold_in(keys[1], 1), TOKENS // TOK_DEV)
    routes_turns = jax.random.permutation(jax.random.fold_in(keys[1], 3), TOKENS // TOK_DEV)
    routes = jax.vmap(lambda own, number: assign_block(jax.random.fold_in(keys[1], 2), own, number, TOK_DEV, EXPERTS, TOP, CAP, 1))(routes_keys, routes_turns).reshape((TOKENS, TOP))
    route_weights = jnp.clip(0.1 + 0.9 * jax.random.uniform(keys[2], (TOKENS, TOP), jnp.float32) ** levels(keys[2], (TOKENS, TOP), ((0, 16),), -0.2, 0.2), 0.1, 1.0)
    learner_weights = draw_learner_weights(jax.random.fold_in(keys[4], 71), 0)
    return {"tokens": tokens, "routes": routes, "route_weights": route_weights, "learner_weights": learner_weights}


def reference(tokens, routes, route_weights, learner_weights):
    block_ids = routes.reshape(N_EXPERT, TOK_DEV * TOP)
    one_hot = (block_ids[:, :, None] == jnp.arange(EXPERTS, dtype=jnp.int32)[None, None, :]).astype(jnp.int32)
    slot_rank = (jnp.sum(jnp.cumsum(one_hot, axis=1) * one_hot, axis=2) - 1).astype(jnp.int32)
    source_of = jnp.broadcast_to(jnp.arange(N_EXPERT, dtype=jnp.int32)[:, None], block_ids.shape)
    token_of = source_of * TOK_DEV + jnp.arange(TOK_DEV * TOP, dtype=jnp.int32)[None, :] // TOP
    slot_list = jnp.full((EXPERTS, N_EXPERT, CAP), TOKENS, jnp.int32).at[block_ids, source_of, slot_rank].set(token_of)
    padded = jnp.concatenate([tokens, jnp.zeros((1, D), tokens.dtype)], axis=0)

    def per_expert(inputs):
        weight, listed = inputs
        gathered_rows = padded[listed.reshape(-1)]
        return jnp.dot(gathered_rows, weight, preferred_element_type=jnp.float32).astype(jnp.bfloat16)

    outputs = lax.map(per_expert, (learner_weights, slot_list))
    picked = outputs.reshape(EXPERTS, N_EXPERT, CAP, FF)[block_ids, source_of, slot_rank]
    weights = route_weights.reshape(N_EXPERT, TOK_DEV * TOP, 1)
    combined = jnp.sum((picked.astype(jnp.float32) * weights).reshape(TOKENS, TOP, FF), axis=1).astype(jnp.bfloat16)
    expert_amax = jnp.max(jnp.abs(learner_weights), axis=(1, 2)).astype(jnp.float32)
    return combined, expert_amax
```

```python
import jax
import jax.numpy as jnp
from jax import lax
from jax.sharding import PartitionSpec as P


def shards(tokens, routes, route_weights, learner_weights):
    n = lax.axis_size("expert")
    rows, width = tokens.shape
    experts, depth, ff = learner_weights.shape
    local_max = lax.pmax(
        jnp.max(jnp.abs(learner_weights), axis=(1, 2)).astype(jnp.float32), "tensor"
    )
    chosen = routes[:, :, None] == jnp.arange(experts, dtype=jnp.int32)
    gate = jnp.sum(jnp.where(chosen, route_weights[:, :, None], 0.0), axis=1)
    high = lax.reduce_precision(gate, 8, 7)
    low = gate - high
    extras = jnp.concatenate([high, low], axis=1).astype(jnp.bfloat16)
    columns = tokens.reshape(rows, n, depth).transpose(1, 0, 2)
    largest = jnp.broadcast_to(local_max.astype(jnp.bfloat16)[:, None, None], (n, rows, 1))
    send = jnp.concatenate(
        [columns, jnp.broadcast_to(extras, (n, rows, 2 * experts)), largest], axis=2
    )
    got = lax.all_to_all(send, "expert", split_axis=0, concat_axis=0, tiled=True)
    expert_amax = jnp.max(got[:, 0, depth + 2 * experts]).astype(jnp.float32).reshape(1)
    x = got[:, :, :depth].reshape(n * rows, depth).astype(jnp.float32)
    extras = got[:, :, depth : depth + 2 * experts].astype(jnp.float32).reshape(n * rows, -1)
    gates = extras[:, :experts] + extras[:, experts:]
    scaled = (x[:, None, :] * gates[:, :, None]).astype(jnp.bfloat16)
    partial = jnp.dot(
        scaled.reshape(n * rows, experts * depth),
        learner_weights.reshape(experts * depth, ff),
        preferred_element_type=jnp.float32,
    ).astype(jnp.bfloat16)
    back = lax.all_to_all(
        partial.reshape(n, rows, ff), "expert", split_axis=0, concat_axis=0, tiled=True
    )
    combined = jnp.sum(back.astype(jnp.float32), axis=0).astype(jnp.bfloat16)
    return (combined, expert_amax)


def solution(mesh):
    return jax.shard_map(
        shards,
        mesh=mesh,
        in_specs=(
            P("expert", None),
            P("expert", None),
            P("expert", None),
            P(None, "expert", "tensor"),
        ),
        out_specs=(P("expert", "tensor"), P("expert")),
        check_vma=False,
    )
```

```python
import functools

import jax
import jax.numpy as jnp
from jax import lax
from jax.experimental import pallas as pl
from jax.experimental.pallas import tpu as pltpu
from jax.sharding import PartitionSpec as P

LANES = 128


def partial_kernel(got_ref, weight_ref, *rest, n, rows, depth, experts, other):
    tail_ref, out_ref, scaled_ref = rest if other else (None, *rest)
    half = n // 2
    ff = weight_ref.shape[1]
    mine = (lax.axis_index("expert") >= half).astype(jnp.int32)
    first = (1 - mine if other else mine) * half
    step = max(1, 64 // rows)
    for r in range(0, half, step):
        count = step * rows
        block = got_ref[pl.ds(first + r, step)].reshape(count, -1)
        x = block[:, :depth].astype(jnp.float32)
        extras = block[:, depth:].astype(jnp.float32)
        gates = extras[:, :experts] + extras[:, experts : 2 * experts]
        for e in range(experts):
            scaled_ref[r * rows : r * rows + count, e * depth : (e + 1) * depth] = (
                x * gates[:, e : e + 1]
            ).astype(jnp.bfloat16)
    product = jnp.dot(scaled_ref[...], weight_ref[...], preferred_element_type=jnp.float32)
    out_ref[:, :, :ff] = product.astype(jnp.bfloat16).reshape(half, rows, ff)
    if other:
        out_ref[:, :, ff:] = tail_ref[...]


def partials(got, weight, tail, n, rows, depth, experts):
    half, ff = n // 2, weight.shape[1]
    width = ff + (0 if tail is None else tail.shape[2])
    operands = (got, weight) if tail is None else (got, weight, tail)
    return pl.pallas_call(
        functools.partial(
            partial_kernel,
            n=n,
            rows=rows,
            depth=depth,
            experts=experts,
            other=tail is not None,
        ),
        out_shape=jax.ShapeDtypeStruct((half, rows, width), jnp.bfloat16),
        in_specs=[pl.BlockSpec(memory_space=pltpu.VMEM)] * len(operands),
        out_specs=pl.BlockSpec(memory_space=pltpu.VMEM),
        scratch_shapes=[pltpu.VMEM((half * rows, experts * depth), jnp.bfloat16)],
        compiler_params=pltpu.CompilerParams(vmem_limit_bytes=24 << 20),
        cost_estimate=pl.CostEstimate(
            flops=2 * half * rows * experts * depth * ff,
            bytes_accessed=weight.size * 2,
            transcendentals=0,
        ),
    )(*operands)


def plain_partials(got, weight, tail, n, rows, depth, experts):
    half, ff = n // 2, weight.shape[1]
    mine = (lax.axis_index("expert") >= half).astype(jnp.int32)
    first = (mine if tail is None else 1 - mine) * half
    blocks = lax.dynamic_slice_in_dim(got, first, half, 0)

    def one(block):
        block = block.astype(jnp.float32)
        gates = block[:, depth : depth + experts] + block[:, depth + experts : depth + 2 * experts]
        scaled = (block[:, None, :depth] * gates[:, :, None]).astype(jnp.bfloat16)
        product = jnp.dot(
            scaled.reshape(rows, experts * depth), weight, preferred_element_type=jnp.float32
        )
        return product.astype(jnp.bfloat16)

    out = lax.map(one, blocks)
    return out if tail is None else jnp.concatenate([out, tail], axis=2)


def shards(tokens, routes, route_weights, learner_weights):
    n, pair = lax.axis_size("expert"), lax.axis_size("tensor")
    rows, width = tokens.shape
    experts, depth, ff = learner_weights.shape
    half = n // 2
    halves = [list(range(half)), list(range(half, n))]
    weight = learner_weights.reshape(experts * depth, ff)
    chosen = routes[:, :, None] == jnp.arange(experts, dtype=jnp.int32)
    gate = jnp.sum(jnp.where(chosen, route_weights[:, :, None], 0.0), axis=1)
    high = lax.reduce_precision(gate, 8, 7)
    low = gate - high
    extras = jnp.concatenate([high, low], axis=1).astype(jnp.bfloat16)
    extras = jnp.pad(extras, ((0, 0), (0, -(2 * experts) % LANES)))
    columns = tokens.reshape(rows, n, depth).transpose(1, 0, 2)
    send = jnp.concatenate([columns, jnp.broadcast_to(extras, (n, *extras.shape))], axis=2)
    got = lax.all_to_all(send, "expert", split_axis=0, concat_axis=0, tiled=True)
    largest = jnp.max(jnp.abs(learner_weights), axis=(1, 2))
    if pair == 2:
        largest = jnp.maximum(largest, lax.ppermute(largest, "tensor", [(0, 1), (1, 0)]))
    else:
        largest = lax.pmax(largest, "tensor")
    mine = (lax.axis_index("expert") >= half).astype(jnp.int32)
    theirs_max = lax.dynamic_slice_in_dim(largest, (1 - mine) * half, half, 0)
    mine_max = lax.dynamic_slice_in_dim(largest, mine * half, half, 0)
    tail = jnp.concatenate(
        [
            jnp.broadcast_to(part[:, None, None], (half, rows // 2, LANES))
            for part in (theirs_max, mine_max)
        ],
        axis=1,
    )
    compute = partials if depth % LANES == 0 and ff % LANES == 0 else plain_partials
    shape = (n, rows, depth, experts)
    other = compute(got, weight, tail, *shape)
    other = lax.all_to_all(
        other, "expert", split_axis=0, concat_axis=0, tiled=True, axis_index_groups=halves
    )
    near = compute(got, weight, None, *shape)
    near = lax.all_to_all(
        near, "expert", split_axis=0, concat_axis=0, tiled=True, axis_index_groups=halves
    )
    merged_max = jnp.max(other[:, :, ff:], axis=0)
    merged = jnp.sum(other[:, :, :ff].astype(jnp.float32), axis=0).astype(jnp.bfloat16)
    merged = jnp.concatenate([merged, merged_max], axis=1)
    crossed = lax.ppermute(merged, "expert", [(i, (i + half) % n) for i in range(n)])
    combined = jnp.sum(near.astype(jnp.float32), axis=0) + crossed[:, :ff].astype(jnp.float32)
    expert_amax = jnp.maximum(merged_max[rows - 1, :1], crossed[0, ff : ff + 1])
    return (combined.astype(jnp.bfloat16), expert_amax.astype(jnp.float32))


def solution(mesh):
    return jax.shard_map(
        shards,
        mesh=mesh,
        in_specs=(
            P("expert", None),
            P("expert", None),
            P("expert", None),
            P(None, "expert", "tensor"),
        ),
        out_specs=(P("expert", "tensor"), P("expert")),
        check_vma=False,
    )
```

```python
import functools

import jax
import jax.numpy as jnp
from jax import lax
from jax.experimental import pallas as pl
from jax.experimental.pallas import tpu as pltpu
from jax.sharding import PartitionSpec as P

LANES = 128
SUBLANES = 8
VMEM = pl.BlockSpec(memory_space=pltpu.VMEM)
HBM = pl.BlockSpec(memory_space=pltpu.HBM)
TILE = 256


def params(mebibytes):
    return pltpu.CompilerParams(vmem_limit_bytes=mebibytes << 20)


def pack_kernel(tokens_ref, routes_ref, weights_ref, send_ref, routes_buf, weights_buf, sem):
    n, _, depth = send_ref.shape
    choices, rows = routes_ref.shape
    copies = [
        pltpu.make_async_copy(routes_ref, routes_buf, sem.at[n]),
        pltpu.make_async_copy(weights_ref, weights_buf, sem.at[n + 1]),
    ]
    copies += [
        pltpu.make_async_copy(
            tokens_ref.at[:, pl.ds(i * depth, depth)], send_ref.at[i, pl.ds(0, rows)], sem.at[i]
        )
        for i in range(n)
    ]
    for copy in copies:
        copy.start()
    for copy in copies[:2]:
        copy.wait()
    expert = lax.broadcasted_iota(jnp.int32, (n, rows), 0)
    gate = jnp.zeros((n, rows), jnp.float32)
    for k in range(choices):
        chosen = routes_buf[k : k + 1, :] == expert
        gate += jnp.where(chosen, weights_buf[k : k + 1, :], 0.0)
    gate = gate.T
    high = gate.astype(jnp.bfloat16).astype(jnp.float32)
    low = gate - high
    terms = []
    for r in range(0, rows, SUBLANES):
        terms += [high[r : r + SUBLANES], low[r : r + SUBLANES]]
    spare = depth - len(terms) * n
    if spare:
        terms.append(jnp.zeros((SUBLANES, spare), jnp.float32))
    packed = jnp.concatenate(terms, axis=1).astype(jnp.bfloat16)
    for i in range(n):
        send_ref[i, rows:, :] = packed
    for copy in copies[2:]:
        copy.wait()


def pack(tokens, routes, route_weights, n, depth):
    rows, choices = routes.shape
    return pl.pallas_call(
        pack_kernel,
        out_shape=jax.ShapeDtypeStruct((n, rows + SUBLANES, depth), jnp.bfloat16),
        in_specs=[HBM] * 3,
        out_specs=VMEM,
        scratch_shapes=[
            pltpu.VMEM((choices, rows), jnp.int32),
            pltpu.VMEM((choices, rows), jnp.float32),
            pltpu.SemaphoreType.DMA((n + 2,)),
        ],
        compiler_params=params(60),
    )(tokens, routes.T, route_weights.T)


def largest_kernel(weight_ref, held_ref, largest_ref, rest_ref, sem):
    experts = weight_ref.shape[0]
    kept = held_ref.shape[0]
    places = [held_ref.at[e] if e < kept else rest_ref.at[e - kept] for e in range(experts)]
    copies = [
        pltpu.make_async_copy(weight_ref.at[e], place, sem.at[e]) for e, place in enumerate(places)
    ]
    for copy in copies:
        copy.start()
    for e, copy in enumerate(copies):
        copy.wait()
        block = jnp.abs(places[e][...].astype(jnp.float32))
        row = jnp.max(block, axis=0, keepdims=True)
        top = jnp.max(row, axis=1, keepdims=True)
        largest_ref[e : e + 1, :] = jnp.broadcast_to(top, (1, LANES))


def hold(weights):
    experts, depth, ff = weights.shape
    kept = experts // 2
    return pl.pallas_call(
        largest_kernel,
        out_shape=(
            pltpu.VMEM((kept, depth, ff), weights.dtype),
            jax.ShapeDtypeStruct((experts, LANES), jnp.float32),
        ),
        in_specs=[HBM],
        out_specs=(VMEM, VMEM),
        scratch_shapes=[
            pltpu.VMEM((experts - kept, depth, ff), weights.dtype),
            pltpu.SemaphoreType.DMA((experts,)),
        ],
        compiler_params=params(12),
        cost_estimate=pl.CostEstimate(
            flops=2 * weights.size, bytes_accessed=2 * weights.size, transcendentals=0
        ),
    )(pltpu.with_memory_space_constraint(weights, pltpu.HBM))


def partial_kernel(got_ref, weight_ref, *rest, rows, experts, other):
    if other:
        held_ref, tail_ref, out_ref, scaled_ref, total_ref, rest_ref, sem = rest
        parts = [held_ref, rest_ref.at[0]]
    else:
        out_ref, scaled_ref, total_ref, rest_ref, sem = rest
        parts = [rest_ref.at[0], rest_ref.at[1]]
    n, _, depth = got_ref.shape
    half, ff = n // 2, weight_ref.shape[1]
    mine = (lax.axis_index("expert") >= half).astype(jnp.int32) * half
    theirs = half - mine
    first = theirs if other else mine
    deep = experts // 2 * depth
    copies = [
        None
        if other and i == 0
        else pltpu.make_async_copy(weight_ref.at[pl.ds(i * deep, deep)], part, sem.at[i])
        for i, part in enumerate(parts)
    ]
    for copy in copies:
        if copy is not None:
            copy.start()
    step = max(1, 64 // rows)
    for r in range(0, half, step):
        count = step * rows
        block = got_ref[pl.ds(first + r, step)]
        x = block[:, :rows].reshape(count, depth).astype(jnp.float32)
        packed = block[:, rows:].astype(jnp.float32)
        gates = jnp.concatenate(
            [
                packed[:, :, at : at + experts] + packed[:, :, at + experts : at + 2 * experts]
                for at in range(0, rows // SUBLANES * 2 * experts, 2 * experts)
            ],
            axis=1,
        ).reshape(count, experts)
        for e in range(experts):
            scaled_ref[r * rows : r * rows + count, e * depth : (e + 1) * depth] = (
                x * gates[:, e : e + 1]
            ).astype(jnp.bfloat16)
    for i, (part, copy) in enumerate(zip(parts, copies)):
        if copy is not None:
            copy.wait()
        for at in range(0, ff, TILE):
            product = jnp.dot(
                scaled_ref[:, i * deep : (i + 1) * deep],
                part[:, at : at + TILE],
                preferred_element_type=jnp.float32,
            )
            if i == 0:
                total_ref[:, at : at + TILE] = product
            else:
                product += total_ref[:, at : at + TILE]
                out_ref[:, :, at : at + TILE] = product.astype(jnp.bfloat16).reshape(
                    half, rows, TILE
                )
    if other:
        for r in range(half):
            for at, owner in ((0, theirs + r), (rows // 2, mine + r)):
                out_ref[r, at : at + rows // 2, ff:] = jnp.broadcast_to(
                    tail_ref[pl.ds(owner, 1), :], (rows // 2, LANES)
                ).astype(jnp.bfloat16)


def partials(got, weight, held, tail, rows, experts):
    n, _, depth = got.shape
    half, ff = n // 2, weight.shape[1]
    deep = experts // 2 * depth
    other = held is not None
    operands = (got, pltpu.with_memory_space_constraint(weight, pltpu.HBM))
    if other:
        held = pltpu.with_memory_space_constraint(held.reshape(deep, ff), pltpu.VMEM)
        operands += (held, tail)
    return pl.pallas_call(
        functools.partial(partial_kernel, rows=rows, experts=experts, other=other),
        out_shape=jax.ShapeDtypeStruct((half, rows, ff + LANES * other), jnp.bfloat16),
        in_specs=[VMEM, HBM, VMEM, VMEM][: len(operands)],
        out_specs=VMEM,
        scratch_shapes=[
            pltpu.VMEM((half * rows, experts * depth), jnp.bfloat16),
            pltpu.VMEM((half * rows, ff), jnp.float32),
            pltpu.VMEM((1 if other else 2, deep, ff), weight.dtype),
            pltpu.SemaphoreType.DMA((2,)),
        ],
        compiler_params=params(24),
        cost_estimate=pl.CostEstimate(
            flops=2 * half * rows * experts * depth * ff,
            bytes_accessed=2 * weight.size,
            transcendentals=0,
        ),
    )(*operands)


def finish_kernel(near_ref, merged_ref, crossed_ref, out_ref, largest_ref):
    rows, ff = out_ref.shape
    total = crossed_ref[:, :ff].astype(jnp.float32)
    for i in range(near_ref.shape[0]):
        total += near_ref[i].astype(jnp.float32)
    out_ref[...] = total.astype(jnp.bfloat16)
    own = merged_ref[rows // 2 :, ff:].astype(jnp.float32)
    theirs = crossed_ref[: rows // 2, ff:].astype(jnp.float32)
    largest_ref[0] = jnp.max(jnp.maximum(own, theirs))


def finish(near, merged, crossed):
    _, rows, ff = near.shape
    return pl.pallas_call(
        finish_kernel,
        out_shape=(
            jax.ShapeDtypeStruct((rows, ff), jnp.bfloat16),
            jax.ShapeDtypeStruct((1,), jnp.float32),
        ),
        in_specs=[VMEM] * 3,
        out_specs=(VMEM, pl.BlockSpec(memory_space=pltpu.SMEM)),
        compiler_params=params(8),
    )(near, merged, crossed)


def halves_of(n):
    return [list(range(n // 2)), list(range(n // 2, n))]


def exchange(block, groups=None):
    return lax.all_to_all(
        block, "expert", split_axis=0, concat_axis=0, tiled=True, axis_index_groups=groups
    )


def over_tensor(largest):
    if lax.axis_size("tensor") == 2:
        return jnp.maximum(largest, lax.ppermute(largest, "tensor", [(0, 1), (1, 0)]))
    return lax.pmax(largest, "tensor")


def kernels(tokens, routes, route_weights, learner_weights):
    n = lax.axis_size("expert")
    rows = tokens.shape[0]
    experts, depth, ff = learner_weights.shape
    got = exchange(pack(tokens, routes, route_weights, n, depth))
    held, largest = hold(learner_weights)
    largest = over_tensor(largest)
    weight = learner_weights.reshape(experts * depth, ff)
    other = exchange(partials(got, weight, held, largest, rows, experts), halves_of(n))
    near = exchange(partials(got, weight, None, None, rows, experts), halves_of(n))
    merged_max = jnp.max(other[:, :, ff:], axis=0)
    merged = jnp.sum(other[:, :, :ff].astype(jnp.float32), axis=0).astype(jnp.bfloat16)
    merged = jnp.concatenate([merged, merged_max], axis=1)
    crossed = lax.ppermute(merged, "expert", [(i, (i + n // 2) % n) for i in range(n)])
    return finish(near, merged, crossed)


def plain(tokens, routes, route_weights, learner_weights):
    n = lax.axis_size("expert")
    rows = tokens.shape[0]
    experts, depth, ff = learner_weights.shape
    largest = over_tensor(jnp.max(jnp.abs(learner_weights), axis=(1, 2)))
    chosen = routes[:, :, None] == jnp.arange(experts, dtype=jnp.int32)
    gate = jnp.sum(jnp.where(chosen, route_weights[:, :, None], 0.0), axis=1)
    high = lax.reduce_precision(gate, 8, 7)
    terms = jnp.concatenate([high, gate - high], axis=1).astype(jnp.bfloat16)
    columns = tokens.reshape(rows, n, depth).transpose(1, 0, 2)
    top = jnp.broadcast_to(largest[:, None, None], (n, rows, 1))
    got = exchange(
        jnp.concatenate([columns, jnp.broadcast_to(terms, (n, *terms.shape)), top], axis=2)
    )
    weight = learner_weights.reshape(experts * depth, ff)

    def one(block):
        block = block.astype(jnp.float32)
        gates = block[:, depth : depth + experts] + block[:, depth + experts : depth + 2 * experts]
        scaled = (block[:, None, :depth] * gates[:, :, None]).astype(jnp.bfloat16)
        product = jnp.dot(
            scaled.reshape(rows, experts * depth), weight, preferred_element_type=jnp.float32
        )
        return product.astype(jnp.bfloat16)

    back = exchange(lax.map(one, got))
    combined = jnp.sum(back.astype(jnp.float32), axis=0).astype(jnp.bfloat16)
    expert_amax = jnp.max(got[:, 0, depth + 2 * experts]).astype(jnp.float32).reshape(1)
    return (combined, expert_amax)


def shards(tokens, routes, route_weights, learner_weights):
    n, rows = lax.axis_size("expert"), tokens.shape[0]
    experts, depth, ff = learner_weights.shape
    aligned = depth % LANES == 0 and ff % TILE == 0 and rows % 32 == 0 and n % 2 == 0
    fits = rows // SUBLANES * 2 * experts <= depth
    small = experts * depth * ff <= 4 << 20 and n * rows <= 1024
    form = kernels if aligned and fits and small and experts == n else plain
    return form(tokens, routes, route_weights, learner_weights)


def solution(mesh):
    return jax.shard_map(
        shards,
        mesh=mesh,
        in_specs=(
            P("expert", None),
            P("expert", None),
            P("expert", None),
            P(None, "expert", "tensor"),
        ),
        out_specs=(P("expert", "tensor"), P("expert")),
        check_vma=False,
    )
```

```python
import functools

import jax
import jax.numpy as jnp
from jax import lax
from jax.experimental import pallas as pl
from jax.experimental.pallas import tpu as pltpu
from jax.sharding import PartitionSpec as P

LANES = 128
SUBLANES = 8
VMEM = pl.BlockSpec(memory_space=pltpu.VMEM)
HBM = pl.BlockSpec(memory_space=pltpu.HBM)
TILE = 256


def params(mebibytes):
    return pltpu.CompilerParams(vmem_limit_bytes=mebibytes << 20)


def pack_kernel(
    tokens_ref, routes_ref, weights_ref, send_ref, block_ref, routes_buf, weights_buf, sem, out_sem
):
    n, _, width = block_ref.shape
    choices, rows = routes_ref.shape
    core = lax.axis_index("tensor")
    copies = [
        pltpu.make_async_copy(routes_ref, routes_buf, sem.at[n]),
        pltpu.make_async_copy(weights_ref, weights_buf, sem.at[n + 1]),
    ]
    copies += [
        pltpu.make_async_copy(
            tokens_ref.at[:, pl.ds(pl.multiple_of((2 * (n - 1 - i) + core) * width, LANES), width)],
            block_ref.at[i, pl.ds(0, rows)],
            sem.at[i],
        )
        for i in range(n)
    ]
    for copy in copies:
        copy.start()
    for copy in copies[:2]:
        copy.wait()
    expert = lax.broadcasted_iota(jnp.int32, (n, rows), 0)
    gate = jnp.zeros((n, rows), jnp.float32)
    for k in range(choices):
        chosen = routes_buf[k : k + 1, :] == expert
        gate += jnp.where(chosen, weights_buf[k : k + 1, :], 0.0)
    gate = gate.T
    high = gate.astype(jnp.bfloat16).astype(jnp.float32)
    low = gate - high
    terms = []
    for r in range(0, rows, SUBLANES):
        terms += [high[r : r + SUBLANES], low[r : r + SUBLANES]]
    spare = width - len(terms) * n
    if spare:
        terms.append(jnp.zeros((SUBLANES, spare), jnp.float32))
    packed = jnp.concatenate(terms, axis=1).astype(jnp.bfloat16)
    for i in range(n):
        block_ref[i, rows:, :] = packed
    group = n // 4
    outs = []
    for i in range(4):
        part = pl.ds(i * group, group)
        for copy in copies[2 + i * group : 2 + (i + 1) * group]:
            copy.wait()
        outs.append(pltpu.make_async_copy(block_ref.at[part], send_ref.at[part], out_sem.at[i]))
        outs[-1].start()
    for out in outs:
        out.wait()


def pack(tokens, routes, route_weights, n, width):
    rows, choices = routes.shape
    shape = (n, rows + SUBLANES, width)
    operands = (tokens, routes.T, route_weights.T)
    return pl.pallas_call(
        pack_kernel,
        out_shape=pltpu.HBM(shape, jnp.bfloat16),
        in_specs=[HBM] * 3,
        out_specs=HBM,
        scratch_shapes=[
            pltpu.VMEM(shape, jnp.bfloat16),
            pltpu.VMEM((choices, rows), jnp.int32),
            pltpu.VMEM((choices, rows), jnp.float32),
            pltpu.SemaphoreType.DMA((n + 2,)),
            pltpu.SemaphoreType.DMA((4,)),
        ],
        compiler_params=params(8),
    )(*(pltpu.with_memory_space_constraint(operand, pltpu.HBM) for operand in operands))


def largest_kernel(weight_ref, held_ref, largest_ref, rest_ref, sem):
    experts = weight_ref.shape[0]
    kept = held_ref.shape[0]
    places = [held_ref.at[e] if e < kept else rest_ref.at[e - kept] for e in range(experts)]
    copies = [
        pltpu.make_async_copy(weight_ref.at[e], place, sem.at[e]) for e, place in enumerate(places)
    ]
    for copy in copies:
        copy.start()
    for e, copy in enumerate(copies):
        copy.wait()
        block = jnp.abs(places[e][...].astype(jnp.float32))
        row = jnp.max(block, axis=0, keepdims=True)
        top = jnp.max(row, axis=1, keepdims=True)
        largest_ref[e : e + 1, :] = jnp.broadcast_to(top, (1, LANES))


def hold(weights):
    experts, depth, ff = weights.shape
    kept = experts // 2
    return pl.pallas_call(
        largest_kernel,
        out_shape=(
            pltpu.VMEM((kept, depth, ff), weights.dtype),
            jax.ShapeDtypeStruct((experts, LANES), jnp.float32),
        ),
        in_specs=[HBM],
        out_specs=(VMEM, VMEM),
        scratch_shapes=[
            pltpu.VMEM((experts - kept, depth, ff), weights.dtype),
            pltpu.SemaphoreType.DMA((experts,)),
        ],
        compiler_params=params(12),
        cost_estimate=pl.CostEstimate(
            flops=2 * weights.size, bytes_accessed=2 * weights.size, transcendentals=0
        ),
    )(pltpu.with_memory_space_constraint(weights, pltpu.HBM))


def partial_kernel(kept_ref, swapped_ref, weight_ref, *rest, rows, experts, other):
    if other:
        held_ref, tail_ref, out_ref, scaled_ref, total_ref, rest_ref, block_ref, sem, out_sem = rest
        parts = [held_ref, rest_ref.at[0]]
    else:
        out_ref, scaled_ref, total_ref, rest_ref, block_ref, sem, out_sem = rest
        parts = [rest_ref.at[0], rest_ref.at[1]]
    n, _, width = kept_ref.shape
    half, ff, depth = n // 2, weight_ref.shape[1], 2 * width
    mine = (lax.axis_index("expert") >= half).astype(jnp.int32) * half
    theirs = half - mine
    first = mine if other else theirs
    left = lax.axis_index("tensor") == 0
    deep = experts // 2 * depth
    copies = [
        None
        if other and i == 0
        else pltpu.make_async_copy(weight_ref.at[pl.ds(i * deep, deep)], part, sem.at[i])
        for i, part in enumerate(parts)
    ]
    for copy in copies:
        if copy is not None:
            copy.start()
    outs = []

    def send(at, size):
        lanes = pl.ds(at, size)
        outs.append(
            pltpu.make_async_copy(
                block_ref.at[:, :, lanes], out_ref.at[:, :, lanes], out_sem.at[len(outs)]
            )
        )
        outs[-1].start()

    if other:
        for r in range(half):
            for at, owner in ((0, theirs + half - 1 - r), (rows // 2, mine + half - 1 - r)):
                block_ref[r, at : at + rows // 2, ff:] = jnp.broadcast_to(
                    tail_ref[pl.ds(owner, 1), :], (rows // 2, LANES)
                ).astype(jnp.bfloat16)
        send(ff, LANES)
    step = max(1, 64 // rows)
    for r in range(0, half, step):
        count = step * rows
        kept = kept_ref[pl.ds(first + r, step)].astype(jnp.float32)
        swapped = swapped_ref[pl.ds(first + r, step), :rows].astype(jnp.float32)
        own = kept[:, :rows]
        x = jnp.concatenate(
            [jnp.where(left, own, swapped), jnp.where(left, swapped, own)], axis=2
        ).reshape(count, depth)
        packed = kept[:, rows:]
        gates = jnp.concatenate(
            [
                packed[:, :, at : at + experts] + packed[:, :, at + experts : at + 2 * experts]
                for at in range(0, rows // SUBLANES * 2 * experts, 2 * experts)
            ],
            axis=1,
        ).reshape(count, experts)
        for e in range(experts):
            scaled_ref[r * rows : r * rows + count, e * depth : (e + 1) * depth] = (
                x * gates[:, e : e + 1]
            ).astype(jnp.bfloat16)
    for i, (part, copy) in enumerate(zip(parts, copies)):
        if copy is not None:
            copy.wait()
        for at in range(0, ff, TILE):
            product = jnp.dot(
                scaled_ref[:, i * deep : (i + 1) * deep],
                part[:, at : at + TILE],
                preferred_element_type=jnp.float32,
            )
            if i == 0:
                total_ref[:, at : at + TILE] = product
            else:
                product += total_ref[:, at : at + TILE]
                block_ref[:, :, at : at + TILE] = product.astype(jnp.bfloat16).reshape(
                    half, rows, TILE
                )
                send(at, TILE)
    for out in outs:
        out.wait()


def partials(got, weight, held, tail, rows, experts):
    n, _, width = got[0].shape
    half, ff, depth = n // 2, weight.shape[1], 2 * width
    deep = experts // 2 * depth
    other = held is not None
    operands = (*got, pltpu.with_memory_space_constraint(weight, pltpu.HBM))
    if other:
        held = pltpu.with_memory_space_constraint(held.reshape(deep, ff), pltpu.VMEM)
        operands += (held, tail)
    shape = (half, rows, ff + LANES * other)
    return pl.pallas_call(
        functools.partial(partial_kernel, rows=rows, experts=experts, other=other),
        out_shape=pltpu.HBM(shape, jnp.bfloat16),
        in_specs=[VMEM, VMEM, HBM, VMEM, VMEM][: len(operands)],
        out_specs=HBM,
        scratch_shapes=[
            pltpu.VMEM((half * rows, experts * depth), jnp.bfloat16),
            pltpu.VMEM((half * rows, ff), jnp.float32),
            pltpu.VMEM((1 if other else 2, deep, ff), weight.dtype),
            pltpu.VMEM(shape, jnp.bfloat16),
            pltpu.SemaphoreType.DMA((2,)),
            pltpu.SemaphoreType.DMA((ff // TILE + 1,)),
        ],
        compiler_params=params(24),
        cost_estimate=pl.CostEstimate(
            flops=2 * half * rows * experts * depth * ff,
            bytes_accessed=2 * weight.size,
            transcendentals=0,
        ),
    )(*operands)


def finish_kernel(near_ref, merged_ref, crossed_ref, out_ref, largest_ref):
    rows, ff = out_ref.shape
    total = crossed_ref[:, :ff].astype(jnp.float32)
    for i in range(near_ref.shape[0]):
        total += near_ref[i].astype(jnp.float32)
    out_ref[...] = total.astype(jnp.bfloat16)
    own = merged_ref[rows // 2 :, ff:].astype(jnp.float32)
    theirs = crossed_ref[: rows // 2, ff:].astype(jnp.float32)
    largest_ref[0] = jnp.max(jnp.maximum(own, theirs))


def finish(near, merged, crossed):
    _, rows, ff = near.shape
    return pl.pallas_call(
        finish_kernel,
        out_shape=(
            jax.ShapeDtypeStruct((rows, ff), jnp.bfloat16),
            jax.ShapeDtypeStruct((1,), jnp.float32),
        ),
        in_specs=[VMEM] * 3,
        out_specs=(VMEM, pl.BlockSpec(memory_space=pltpu.SMEM)),
        compiler_params=params(8),
    )(near, merged, crossed)


def exchange(block, parts):
    n = lax.axis_size("expert")
    size = n // parts
    groups = [list(range(first + size - 1, first - 1, -1)) for first in range(0, n, size)]
    return lax.all_to_all(
        block, "expert", split_axis=0, concat_axis=0, tiled=True, axis_index_groups=groups
    )


def over_tensor(largest):
    if lax.axis_size("tensor") == 2:
        return jnp.maximum(largest, lax.ppermute(largest, "tensor", [(0, 1), (1, 0)]))
    return lax.pmax(largest, "tensor")


def kernels(tokens, routes, route_weights, learner_weights):
    n = lax.axis_size("expert")
    rows = tokens.shape[0]
    experts, depth, ff = learner_weights.shape
    got = exchange(pack(tokens, routes, route_weights, n, depth // 2), 1)
    held, largest = hold(learner_weights)
    largest = over_tensor(largest)
    got, held, largest = lax.optimization_barrier((got, held, largest))
    got = (got, lax.ppermute(got, "tensor", [(0, 1), (1, 0)]))
    weight = learner_weights.reshape(experts * depth, ff)
    other = exchange(partials(got, weight, held, largest, rows, experts), 2)
    near = exchange(partials(got, weight, None, None, rows, experts), 2)
    merged_max = jnp.max(other[:, :, ff:], axis=0)
    merged = jnp.sum(other[:, :, :ff].astype(jnp.float32), axis=0).astype(jnp.bfloat16)
    merged = jnp.concatenate([merged, merged_max], axis=1)
    crossed = lax.ppermute(merged, "expert", [(i, (i + n // 2) % n) for i in range(n)])
    return finish(near, merged, crossed)


def plain(tokens, routes, route_weights, learner_weights):
    n = lax.axis_size("expert")
    rows = tokens.shape[0]
    experts, depth, ff = learner_weights.shape
    largest = over_tensor(jnp.max(jnp.abs(learner_weights), axis=(1, 2)))
    chosen = routes[:, :, None] == jnp.arange(experts, dtype=jnp.int32)
    gate = jnp.sum(jnp.where(chosen, route_weights[:, :, None], 0.0), axis=1)
    high = lax.reduce_precision(gate, 8, 7)
    terms = jnp.concatenate([high, gate - high], axis=1).astype(jnp.bfloat16)
    columns = tokens.reshape(rows, n, depth).transpose(1, 0, 2)[::-1]
    top = jnp.broadcast_to(largest[::-1, None, None], (n, rows, 1))
    got = exchange(
        jnp.concatenate([columns, jnp.broadcast_to(terms, (n, *terms.shape)), top], axis=2), 1
    )
    weight = learner_weights.reshape(experts * depth, ff)

    def one(block):
        block = block.astype(jnp.float32)
        gates = block[:, depth : depth + experts] + block[:, depth + experts : depth + 2 * experts]
        scaled = (block[:, None, :depth] * gates[:, :, None]).astype(jnp.bfloat16)
        product = jnp.dot(
            scaled.reshape(rows, experts * depth), weight, preferred_element_type=jnp.float32
        )
        return product.astype(jnp.bfloat16)

    back = exchange(lax.map(one, got), 1)
    combined = jnp.sum(back.astype(jnp.float32), axis=0).astype(jnp.bfloat16)
    expert_amax = jnp.max(got[:, 0, depth + 2 * experts]).astype(jnp.float32).reshape(1)
    return (combined, expert_amax)


def shards(tokens, routes, route_weights, learner_weights):
    n, rows = lax.axis_size("expert"), tokens.shape[0]
    experts, depth, ff = learner_weights.shape
    aligned = depth % (2 * LANES) == 0 and ff % TILE == 0 and rows % 32 == 0 and n % 4 == 0
    fits = lax.axis_size("tensor") == 2 and rows // SUBLANES * 2 * experts <= depth // 2
    small = experts * depth * ff <= 4 << 20 and n * rows <= 1024
    form = kernels if aligned and fits and small and experts == n else plain
    return form(tokens, routes, route_weights, learner_weights)


def solution(mesh):
    return jax.shard_map(
        shards,
        mesh=mesh,
        in_specs=(
            P("expert", None),
            P("expert", None),
            P("expert", None),
            P(None, "expert", "tensor"),
        ),
        out_specs=(P("expert", "tensor"), P("expert")),
        check_vma=False,
    )
```

```python
import functools

import jax
import jax.numpy as jnp
from jax import lax
from jax.experimental import pallas as pl
from jax.experimental.pallas import tpu as pltpu
from jax.sharding import PartitionSpec as P

LANES = 128
SUBLANES = 8
PLANE = 4
VMEM = pl.BlockSpec(memory_space=pltpu.VMEM)
HBM = pl.BlockSpec(memory_space=pltpu.HBM)
TILE = 256


def params(mebibytes):
    return pltpu.CompilerParams(vmem_limit_bytes=mebibytes << 20)


def pack_kernel(
    tokens_ref, routes_ref, weights_ref, send_ref, block_ref, routes_buf, weights_buf, sem, out_sem
):
    n, _, width = block_ref.shape
    choices, rows = routes_ref.shape
    core = lax.axis_index("tensor")
    copies = [
        pltpu.make_async_copy(routes_ref, routes_buf, sem.at[n]),
        pltpu.make_async_copy(weights_ref, weights_buf, sem.at[n + 1]),
    ]
    copies += [
        pltpu.make_async_copy(
            tokens_ref.at[:, pl.ds(pl.multiple_of((2 * (n - 1 - i) + core) * width, LANES), width)],
            block_ref.at[i, pl.ds(0, rows)],
            sem.at[i],
        )
        for i in range(n)
    ]
    for copy in copies:
        copy.start()
    for copy in copies[:2]:
        copy.wait()
    expert = lax.broadcasted_iota(jnp.int32, (n, rows), 0)
    gate = jnp.zeros((n, rows), jnp.float32)
    for k in range(choices):
        chosen = routes_buf[k : k + 1, :] == expert
        gate += jnp.where(chosen, weights_buf[k : k + 1, :], 0.0)
    gate = gate.T
    high = gate.astype(jnp.bfloat16).astype(jnp.float32)
    low = gate - high
    terms = []
    for r in range(0, rows, SUBLANES):
        terms += [high[r : r + SUBLANES], low[r : r + SUBLANES]]
    spare = width - len(terms) * n
    if spare:
        terms.append(jnp.zeros((SUBLANES, spare), jnp.float32))
    packed = jnp.concatenate(terms, axis=1).astype(jnp.bfloat16)
    for i in range(n):
        block_ref[i, rows:, :] = packed
    group = n // 4
    outs = []
    for i in range(4):
        part = pl.ds(i * group, group)
        for copy in copies[2 + i * group : 2 + (i + 1) * group]:
            copy.wait()
        outs.append(pltpu.make_async_copy(block_ref.at[part], send_ref.at[part], out_sem.at[i]))
        outs[-1].start()
    for out in outs:
        out.wait()


def pack(tokens, routes, route_weights, n, width):
    rows, choices = routes.shape
    shape = (n, rows + SUBLANES, width)
    operands = (tokens, routes.T, route_weights.T)
    return pl.pallas_call(
        pack_kernel,
        out_shape=pltpu.HBM(shape, jnp.bfloat16),
        in_specs=[HBM] * 3,
        out_specs=HBM,
        scratch_shapes=[
            pltpu.VMEM(shape, jnp.bfloat16),
            pltpu.VMEM((choices, rows), jnp.int32),
            pltpu.VMEM((choices, rows), jnp.float32),
            pltpu.SemaphoreType.DMA((n + 2,)),
            pltpu.SemaphoreType.DMA((4,)),
        ],
        compiler_params=params(8),
    )(*(pltpu.with_memory_space_constraint(operand, pltpu.HBM) for operand in operands))


def largest_kernel(weight_ref, held_ref, largest_ref, rest_ref, sem):
    experts = weight_ref.shape[0]
    kept = held_ref.shape[0]
    places = [held_ref.at[e] if e < kept else rest_ref.at[e - kept] for e in range(experts)]
    copies = [
        pltpu.make_async_copy(weight_ref.at[e], place, sem.at[e]) for e, place in enumerate(places)
    ]
    for copy in copies:
        copy.start()
    for e, copy in enumerate(copies):
        copy.wait()
        block = jnp.abs(places[e][...].astype(jnp.float32))
        row = jnp.max(block, axis=0, keepdims=True)
        top = jnp.max(row, axis=1, keepdims=True)
        largest_ref[e : e + 1, :] = jnp.broadcast_to(top, (1, LANES))


def hold(weights):
    experts, depth, ff = weights.shape
    kept = experts // 2
    return pl.pallas_call(
        largest_kernel,
        out_shape=(
            pltpu.VMEM((kept, depth, ff), weights.dtype),
            jax.ShapeDtypeStruct((experts, LANES), jnp.float32),
        ),
        in_specs=[HBM],
        out_specs=(VMEM, VMEM),
        scratch_shapes=[
            pltpu.VMEM((experts - kept, depth, ff), weights.dtype),
            pltpu.SemaphoreType.DMA((experts,)),
        ],
        compiler_params=params(12),
        cost_estimate=pl.CostEstimate(
            flops=2 * weights.size, bytes_accessed=2 * weights.size, transcendentals=0
        ),
    )(pltpu.with_memory_space_constraint(weights, pltpu.HBM))


def place(column, plane):
    index = lax.axis_index("expert")
    planes = lax.axis_size("expert") // PLANE
    beyond = lax.rem(lax.div(index, PLANE) + plane, planes)
    return beyond * PLANE + jnp.bitwise_xor(lax.rem(index, PLANE), column)


def partial_kernel(*refs, rows, experts, columns, load):
    kept_ref, swapped_ref, tail_ref, held_ref, rest_ref, *refs = refs
    away = columns != (0,)
    count = len(columns)
    if load:
        weight_ref, (rest_ref, *refs) = rest_ref, refs
    if away:
        out_refs, (scaled_ref, total_ref, block_ref, sem, out_sem) = refs[:count], refs[count:]
    else:
        own_ref, largest_ref, scaled_ref, total_ref, sem = refs
    n, _, width = kept_ref.shape
    ff, depth, planes = held_ref.shape[1], 2 * width, n // PLANE
    chips = [[place(column, plane) for plane in range(planes)] for column in columns]
    left = lax.axis_index("tensor") == 0
    deep = experts // 2 * depth
    if load:
        fetch = pltpu.make_async_copy(weight_ref.at[pl.ds(deep, deep)], rest_ref, sem)
        fetch.start()
    for i, column in enumerate(chips):
        row = lax.broadcasted_iota(jnp.int32, (SUBLANES, LANES), 0)
        top = jnp.zeros((SUBLANES, LANES), jnp.float32)
        for plane, chip in enumerate(column):
            value = jnp.broadcast_to(tail_ref[pl.ds(chip, 1), :], (SUBLANES, LANES))
            top = jnp.where(row == plane, value, top)
        if away:
            block_ref[i, planes * rows :, :LANES] = top.astype(jnp.bfloat16)
            block_ref[i, planes * rows :, LANES:] = jnp.zeros(
                (SUBLANES, ff - LANES), jnp.bfloat16
            )
        else:
            largest_ref[...] = top
    for i, chip in enumerate([chip for column in chips for chip in column]):
        kept = kept_ref[n - 1 - chip].astype(jnp.float32)
        swapped = swapped_ref[n - 1 - chip, :rows].astype(jnp.float32)
        own = kept[:rows]
        x = jnp.concatenate([jnp.where(left, own, swapped), jnp.where(left, swapped, own)], axis=1)
        packed = kept[rows:]
        gates = jnp.concatenate(
            [
                packed[:, at : at + experts] + packed[:, at + experts : at + 2 * experts]
                for at in range(0, rows // SUBLANES * 2 * experts, 2 * experts)
            ],
            axis=0,
        )
        for e in range(experts):
            scaled_ref[i * rows : (i + 1) * rows, e * depth : (e + 1) * depth] = (
                x * gates[:, e : e + 1]
            ).astype(jnp.bfloat16)
    outs = []
    for i, part in enumerate((held_ref, rest_ref)):
        if load and i == 1:
            fetch.wait()
        for at in range(0, ff, TILE):
            product = jnp.dot(
                scaled_ref[:, i * deep : (i + 1) * deep],
                part[:, at : at + TILE],
                preferred_element_type=jnp.float32,
            )
            if i == 0:
                total_ref[:, at : at + TILE] = product
                continue
            product += total_ref[:, at : at + TILE]
            if not away:
                own_ref[:, at : at + TILE] = product
                continue
            lanes = pl.ds(at, TILE)
            for c, out_ref in enumerate(out_refs):
                block_ref[c, : planes * rows, at : at + TILE] = product[
                    c * planes * rows : (c + 1) * planes * rows
                ].astype(jnp.bfloat16)
                outs.append(
                    pltpu.make_async_copy(
                        block_ref.at[c, :, lanes], out_ref.at[:, lanes], out_sem.at[len(outs)]
                    )
                )
                outs[-1].start()
    for out in outs:
        out.wait()


def partials(got, tail, weights, rows, experts, columns, load=False):
    n, _, width = got[0].shape
    depth, planes = 2 * width, n // PLANE
    held, rest = weights
    deep, ff = held.shape
    away = columns != (0,)
    count = planes * rows * len(columns)
    held = pltpu.with_memory_space_constraint(held, pltpu.VMEM)
    rest = pltpu.with_memory_space_constraint(rest, pltpu.HBM if load else pltpu.VMEM)
    operands = (*got, tail, held, rest)
    out_shape, out_specs = (), ()
    if load:
        out_shape += (pltpu.VMEM((deep, ff), rest.dtype),)
        out_specs += (VMEM,)
    scratch = [
        pltpu.VMEM((count, experts * depth), jnp.bfloat16),
        pltpu.VMEM((count, ff), jnp.float32),
    ]
    if away:
        shape = (planes * rows + SUBLANES, ff)
        out_shape += (pltpu.HBM(shape, jnp.bfloat16),) * len(columns)
        out_specs += (HBM,) * len(columns)
        scratch += [
            pltpu.VMEM((len(columns), *shape), jnp.bfloat16),
            pltpu.SemaphoreType.DMA,
            pltpu.SemaphoreType.DMA((ff // TILE * len(columns),)),
        ]
    else:
        out_shape += (
            jax.ShapeDtypeStruct((count, ff), jnp.float32),
            jax.ShapeDtypeStruct((SUBLANES, LANES), jnp.float32),
        )
        out_specs += (VMEM, VMEM)
        scratch += [pltpu.SemaphoreType.DMA]
    return pl.pallas_call(
        functools.partial(
            partial_kernel, rows=rows, experts=experts, columns=columns, load=load
        ),
        out_shape=out_shape,
        in_specs=[VMEM, VMEM, VMEM, VMEM, HBM if load else VMEM],
        out_specs=out_specs,
        scratch_shapes=scratch,
        compiler_params=params(16),
        cost_estimate=pl.CostEstimate(
            flops=2 * count * experts * depth * ff,
            bytes_accessed=4 * held.size,
            transcendentals=0,
        ),
    )(*operands)


def finish_kernel(own_ref, largest_ref, *refs, planes):
    plane_refs, crossed_refs = refs[: PLANE - 1], refs[PLANE - 1 : -2]
    out_ref, top_ref = refs[-2:]
    rows, ff = out_ref.shape
    total = own_ref[:rows]
    top = largest_ref[:1]
    for ref in plane_refs:
        total += ref[:rows].astype(jnp.float32)
        maxima = ref[planes * rows :, :LANES].astype(jnp.float32)
        top = jnp.maximum(top, maxima[:1])
    for ref in crossed_refs:
        total += ref[:, :ff].astype(jnp.float32)
        top = jnp.maximum(top, ref[:, ff:].astype(jnp.float32)[:1])
    out_ref[...] = total.astype(jnp.bfloat16)
    top_ref[0] = jnp.max(top)


def finish(own, largest, near, crossed, rows):
    operands = (own, largest, *near, *crossed)
    return pl.pallas_call(
        functools.partial(finish_kernel, planes=len(crossed) + 1),
        out_shape=(
            jax.ShapeDtypeStruct((rows, own.shape[1]), jnp.bfloat16),
            jax.ShapeDtypeStruct((1,), jnp.float32),
        ),
        in_specs=[VMEM] * len(operands),
        out_specs=(VMEM, pl.BlockSpec(memory_space=pltpu.SMEM)),
        compiler_params=params(8),
    )(*operands)


def exchange(block, parts):
    n = lax.axis_size("expert")
    size = n // parts
    groups = [list(range(first + size - 1, first - 1, -1)) for first in range(0, n, size)]
    return lax.all_to_all(
        block, "expert", split_axis=0, concat_axis=0, tiled=True, axis_index_groups=groups
    )


def over_tensor(largest):
    if lax.axis_size("tensor") == 2:
        return jnp.maximum(largest, lax.ppermute(largest, "tensor", [(0, 1), (1, 0)]))
    return lax.pmax(largest, "tensor")


def kernels(tokens, routes, route_weights, learner_weights):
    n = lax.axis_size("expert")
    rows = tokens.shape[0]
    experts, depth, ff = learner_weights.shape
    got = exchange(pack(tokens, routes, route_weights, n, depth // 2), 1)
    held, largest = hold(learner_weights)
    largest = over_tensor(largest)
    got, held, largest = lax.optimization_barrier((got, held, largest))
    got = (got, lax.ppermute(got, "tensor", [(0, 1), (1, 0)]))
    held = held.reshape(-1, ff)
    weight = learner_weights.reshape(experts * depth, ff)
    rest, far = partials(got, largest, (held, weight), rows, experts, (3,), load=True)
    side, front = partials(got, largest, (held, rest), rows, experts, (1, 2))
    own, own_largest = partials(got, largest, (held, rest), rows, experts, (0,))
    near = [
        lax.ppermute(block, "expert", [(i, i ^ column) for i in range(n)])
        for column, block in ((1, side), (2, front), (3, far))
    ]
    planes = n // PLANE
    crossed = []
    for plane in range(1, planes):
        begin = plane * rows
        total = own[begin : begin + rows]
        top = own_largest[plane]
        for block in near:
            total += block[begin : begin + rows].astype(jnp.float32)
            top = jnp.maximum(top, block[planes * rows + plane, :LANES].astype(jnp.float32))
        merged = jnp.concatenate([total, jnp.broadcast_to(top, (rows, LANES))], axis=1)
        pairs = [(i, (i + plane * PLANE) % n) for i in range(n)]
        crossed.append(lax.ppermute(merged.astype(jnp.bfloat16), "expert", pairs))
    return finish(own, own_largest, near, crossed, rows)


def plain(tokens, routes, route_weights, learner_weights):
    n = lax.axis_size("expert")
    rows = tokens.shape[0]
    experts, depth, ff = learner_weights.shape
    largest = over_tensor(jnp.max(jnp.abs(learner_weights), axis=(1, 2)))
    chosen = routes[:, :, None] == jnp.arange(experts, dtype=jnp.int32)
    gate = jnp.sum(jnp.where(chosen, route_weights[:, :, None], 0.0), axis=1)
    high = lax.reduce_precision(gate, 8, 7)
    terms = jnp.concatenate([high, gate - high], axis=1).astype(jnp.bfloat16)
    columns = tokens.reshape(rows, n, depth).transpose(1, 0, 2)[::-1]
    top = jnp.broadcast_to(largest[::-1, None, None], (n, rows, 1))
    got = exchange(
        jnp.concatenate([columns, jnp.broadcast_to(terms, (n, *terms.shape)), top], axis=2), 1
    )
    weight = learner_weights.reshape(experts * depth, ff)

    def one(block):
        block = block.astype(jnp.float32)
        gates = block[:, depth : depth + experts] + block[:, depth + experts : depth + 2 * experts]
        scaled = (block[:, None, :depth] * gates[:, :, None]).astype(jnp.bfloat16)
        product = jnp.dot(
            scaled.reshape(rows, experts * depth), weight, preferred_element_type=jnp.float32
        )
        return product.astype(jnp.bfloat16)

    back = exchange(lax.map(one, got), 1)
    combined = jnp.sum(back.astype(jnp.float32), axis=0).astype(jnp.bfloat16)
    expert_amax = jnp.max(got[:, 0, depth + 2 * experts]).astype(jnp.float32).reshape(1)
    return (combined, expert_amax)


def shards(tokens, routes, route_weights, learner_weights):
    n, rows = lax.axis_size("expert"), tokens.shape[0]
    experts, depth, ff = learner_weights.shape
    aligned = depth % (2 * LANES) == 0 and ff % TILE == 0 and rows % 32 == 0 and n % PLANE == 0
    fits = lax.axis_size("tensor") == 2 and rows // SUBLANES * 2 * experts <= depth // 2
    small = experts * depth * ff <= 4 << 20 and n * rows <= 1024 and n <= PLANE * SUBLANES
    form = kernels if aligned and fits and small and experts == n else plain
    return form(tokens, routes, route_weights, learner_weights)


def solution(mesh):
    return jax.shard_map(
        shards,
        mesh=mesh,
        in_specs=(
            P("expert", None),
            P("expert", None),
            P("expert", None),
            P(None, "expert", "tensor"),
        ),
        out_specs=(P("expert", "tensor"), P("expert")),
        check_vma=False,
    )
```

```python
import functools

import jax
import jax.numpy as jnp
from jax import lax
from jax.experimental import pallas as pl
from jax.experimental.pallas import tpu as pltpu
from jax.sharding import PartitionSpec as P

LANES = 128
SUBLANES = 8
PLANE = 4
VMEM = pl.BlockSpec(memory_space=pltpu.VMEM)
HBM = pl.BlockSpec(memory_space=pltpu.HBM)
TILE = 256


def params(mebibytes):
    return pltpu.CompilerParams(vmem_limit_bytes=mebibytes << 20)


def pack_kernel(
    tokens_ref, routes_ref, weights_ref, send_ref, block_ref, routes_buf, weights_buf, sem, out_sem
):
    n, _, width = block_ref.shape
    choices, rows = routes_ref.shape
    core = lax.axis_index("tensor")
    copies = [
        pltpu.make_async_copy(routes_ref, routes_buf, sem.at[n]),
        pltpu.make_async_copy(weights_ref, weights_buf, sem.at[n + 1]),
    ]
    copies += [
        pltpu.make_async_copy(
            tokens_ref.at[:, pl.ds(pl.multiple_of((2 * (n - 1 - i) + core) * width, LANES), width)],
            block_ref.at[i, pl.ds(0, rows)],
            sem.at[i],
        )
        for i in range(n)
    ]
    for copy in copies:
        copy.start()
    for copy in copies[:2]:
        copy.wait()
    expert = lax.broadcasted_iota(jnp.int32, (n, rows), 0)
    gate = jnp.zeros((n, rows), jnp.float32)
    for k in range(choices):
        chosen = routes_buf[k : k + 1, :] == expert
        gate += jnp.where(chosen, weights_buf[k : k + 1, :], 0.0)
    gate = gate.T
    high = gate.astype(jnp.bfloat16).astype(jnp.float32)
    low = gate - high
    terms = []
    for r in range(0, rows, SUBLANES):
        terms += [high[r : r + SUBLANES], low[r : r + SUBLANES]]
    spare = width - len(terms) * n
    if spare:
        terms.append(jnp.zeros((SUBLANES, spare), jnp.float32))
    packed = jnp.concatenate(terms, axis=1).astype(jnp.bfloat16)
    for i in range(n):
        block_ref[i, rows:, :] = packed
    group = n // 4
    outs = []
    for i in range(4):
        part = pl.ds(i * group, group)
        for copy in copies[2 + i * group : 2 + (i + 1) * group]:
            copy.wait()
        outs.append(pltpu.make_async_copy(block_ref.at[part], send_ref.at[part], out_sem.at[i]))
        outs[-1].start()
    for out in outs:
        out.wait()


def pack(tokens, routes, route_weights, n, width):
    rows, choices = routes.shape
    shape = (n, rows + SUBLANES, width)
    operands = (tokens, routes.T, route_weights.T)
    return pl.pallas_call(
        pack_kernel,
        out_shape=pltpu.HBM(shape, jnp.bfloat16),
        in_specs=[HBM] * 3,
        out_specs=HBM,
        scratch_shapes=[
            pltpu.VMEM(shape, jnp.bfloat16),
            pltpu.VMEM((choices, rows), jnp.int32),
            pltpu.VMEM((choices, rows), jnp.float32),
            pltpu.SemaphoreType.DMA((n + 2,)),
            pltpu.SemaphoreType.DMA((4,)),
        ],
        compiler_params=params(8),
    )(*(pltpu.with_memory_space_constraint(operand, pltpu.HBM) for operand in operands))


def largest_kernel(weight_ref, held_ref, largest_ref, rest_ref, sem):
    experts = weight_ref.shape[0]
    kept = held_ref.shape[0]
    places = [held_ref.at[e] if e < kept else rest_ref.at[e - kept] for e in range(experts)]
    copies = [
        pltpu.make_async_copy(weight_ref.at[e], place, sem.at[e]) for e, place in enumerate(places)
    ]
    for copy in copies:
        copy.start()
    for e, copy in enumerate(copies):
        copy.wait()
        block = jnp.abs(places[e][...].astype(jnp.float32))
        row = jnp.max(block, axis=0, keepdims=True)
        top = jnp.max(row, axis=1, keepdims=True)
        largest_ref[e : e + 1, :] = jnp.broadcast_to(top, (1, LANES))


def hold(weights):
    experts, depth, ff = weights.shape
    kept = experts // 2
    return pl.pallas_call(
        largest_kernel,
        out_shape=(
            pltpu.VMEM((kept, depth, ff), weights.dtype),
            jax.ShapeDtypeStruct((experts, LANES), jnp.float32),
        ),
        in_specs=[HBM],
        out_specs=(VMEM, VMEM),
        scratch_shapes=[
            pltpu.VMEM((experts - kept, depth, ff), weights.dtype),
            pltpu.SemaphoreType.DMA((experts,)),
        ],
        compiler_params=params(12),
        cost_estimate=pl.CostEstimate(
            flops=2 * weights.size, bytes_accessed=2 * weights.size, transcendentals=0
        ),
    )(pltpu.with_memory_space_constraint(weights, pltpu.HBM))


def place(column, plane):
    index = lax.axis_index("expert")
    planes = lax.axis_size("expert") // PLANE
    beyond = lax.rem(lax.div(index, PLANE) + plane, planes)
    return beyond * PLANE + jnp.bitwise_xor(lax.rem(index, PLANE), column)


def partial_kernel(*refs, rows, experts, columns, load):
    kept_ref, swapped_ref, tail_ref, held_ref, rest_ref, *refs = refs
    away = columns != (0,)
    count = len(columns)
    if load:
        weight_ref, (rest_ref, *refs) = rest_ref, refs
    if away:
        out_refs, (scaled_ref, total_ref, sem) = refs[:count], refs[count:]
    else:
        own_ref, largest_ref, scaled_ref, total_ref, sem = refs
    n, _, width = kept_ref.shape
    ff, depth, planes = held_ref.shape[1], 2 * width, n // PLANE
    chips = [[place(column, plane) for plane in range(planes)] for column in columns]
    left = lax.axis_index("tensor") == 0
    deep = experts // 2 * depth
    if load:
        fetch = pltpu.make_async_copy(weight_ref.at[pl.ds(deep, deep)], rest_ref, sem)
        fetch.start()
    for i, column in enumerate(chips):
        row = lax.broadcasted_iota(jnp.int32, (SUBLANES, LANES), 0)
        top = jnp.zeros((SUBLANES, LANES), jnp.float32)
        for plane, chip in enumerate(column):
            value = jnp.broadcast_to(tail_ref[pl.ds(chip, 1), :], (SUBLANES, LANES))
            top = jnp.where(row == plane, value, top)
        if away:
            out_refs[i][planes * rows :, :LANES] = top.astype(jnp.bfloat16)
            out_refs[i][planes * rows :, LANES:] = jnp.zeros(
                (SUBLANES, ff - LANES), jnp.bfloat16
            )
        else:
            largest_ref[...] = top
    for i, chip in enumerate([chip for column in chips for chip in column]):
        kept = kept_ref[n - 1 - chip].astype(jnp.float32)
        swapped = swapped_ref[n - 1 - chip, :rows].astype(jnp.float32)
        own = kept[:rows]
        x = jnp.concatenate([jnp.where(left, own, swapped), jnp.where(left, swapped, own)], axis=1)
        packed = kept[rows:]
        gates = jnp.concatenate(
            [
                packed[:, at : at + experts] + packed[:, at + experts : at + 2 * experts]
                for at in range(0, rows // SUBLANES * 2 * experts, 2 * experts)
            ],
            axis=0,
        )
        for e in range(experts):
            scaled_ref[i * rows : (i + 1) * rows, e * depth : (e + 1) * depth] = (
                x * gates[:, e : e + 1]
            ).astype(jnp.bfloat16)
    for i, part in enumerate((held_ref, rest_ref)):
        if load and i == 1:
            fetch.wait()
        for at in range(0, ff, TILE):
            product = jnp.dot(
                scaled_ref[:, i * deep : (i + 1) * deep],
                part[:, at : at + TILE],
                preferred_element_type=jnp.float32,
            )
            if i == 0:
                total_ref[:, at : at + TILE] = product
                continue
            product += total_ref[:, at : at + TILE]
            if not away:
                own_ref[:, at : at + TILE] = product
                continue
            for c, out_ref in enumerate(out_refs):
                out_ref[: planes * rows, at : at + TILE] = product[
                    c * planes * rows : (c + 1) * planes * rows
                ].astype(jnp.bfloat16)


def partials(got, tail, weights, rows, experts, columns, load=False):
    n, _, width = got[0].shape
    depth, planes = 2 * width, n // PLANE
    held, rest = weights
    deep, ff = held.shape
    away = columns != (0,)
    count = planes * rows * len(columns)
    held = pltpu.with_memory_space_constraint(held, pltpu.VMEM)
    rest = pltpu.with_memory_space_constraint(rest, pltpu.HBM if load else pltpu.VMEM)
    operands = (*got, tail, held, rest)
    out_shape = (pltpu.VMEM((deep, ff), rest.dtype),) if load else ()
    scratch = [
        pltpu.VMEM((count, experts * depth), jnp.bfloat16),
        pltpu.VMEM((count, ff), jnp.float32),
        pltpu.SemaphoreType.DMA,
    ]
    if away:
        shape = (planes * rows + SUBLANES, ff)
        out_shape += (jax.ShapeDtypeStruct(shape, jnp.bfloat16),) * len(columns)
    else:
        out_shape += (
            jax.ShapeDtypeStruct((count, ff), jnp.float32),
            jax.ShapeDtypeStruct((SUBLANES, LANES), jnp.float32),
        )
    return pl.pallas_call(
        functools.partial(
            partial_kernel, rows=rows, experts=experts, columns=columns, load=load
        ),
        out_shape=out_shape,
        in_specs=[VMEM, VMEM, VMEM, VMEM, HBM if load else VMEM],
        out_specs=(VMEM,) * len(out_shape),
        scratch_shapes=scratch,
        compiler_params=params(16),
        cost_estimate=pl.CostEstimate(
            flops=2 * count * experts * depth * ff,
            bytes_accessed=4 * held.size,
            transcendentals=0,
        ),
    )(*operands)


def finish_kernel(own_ref, largest_ref, *refs, planes):
    plane_refs, crossed_refs = refs[: PLANE - 1], refs[PLANE - 1 : -2]
    out_ref, top_ref = refs[-2:]
    rows, ff = out_ref.shape
    total = own_ref[:rows]
    top = largest_ref[:1]
    for ref in plane_refs:
        total += ref[:rows].astype(jnp.float32)
        maxima = ref[planes * rows :, :LANES].astype(jnp.float32)
        top = jnp.maximum(top, maxima[:1])
    for ref in crossed_refs:
        total += ref[:, :ff].astype(jnp.float32)
        top = jnp.maximum(top, ref[:, ff:].astype(jnp.float32)[:1])
    out_ref[...] = total.astype(jnp.bfloat16)
    top_ref[0] = jnp.max(top)


def finish(own, largest, near, crossed, rows):
    operands = (own, largest, *near, *crossed)
    return pl.pallas_call(
        functools.partial(finish_kernel, planes=len(crossed) + 1),
        out_shape=(
            jax.ShapeDtypeStruct((rows, own.shape[1]), jnp.bfloat16),
            jax.ShapeDtypeStruct((1,), jnp.float32),
        ),
        in_specs=[VMEM] * len(operands),
        out_specs=(VMEM, pl.BlockSpec(memory_space=pltpu.SMEM)),
        compiler_params=params(8),
    )(*operands)


def exchange(block, parts):
    n = lax.axis_size("expert")
    size = n // parts
    groups = [list(range(first + size - 1, first - 1, -1)) for first in range(0, n, size)]
    return lax.all_to_all(
        block, "expert", split_axis=0, concat_axis=0, tiled=True, axis_index_groups=groups
    )


def over_tensor(largest):
    if lax.axis_size("tensor") == 2:
        return jnp.maximum(largest, lax.ppermute(largest, "tensor", [(0, 1), (1, 0)]))
    return lax.pmax(largest, "tensor")


def kernels(tokens, routes, route_weights, learner_weights):
    n = lax.axis_size("expert")
    rows = tokens.shape[0]
    experts, depth, ff = learner_weights.shape
    got = exchange(pack(tokens, routes, route_weights, n, depth // 2), 1)
    held, largest = hold(learner_weights)
    largest = over_tensor(largest)
    got, held, largest = lax.optimization_barrier((got, held, largest))
    got = (got, lax.ppermute(got, "tensor", [(0, 1), (1, 0)]))
    held = held.reshape(-1, ff)
    weight = learner_weights.reshape(experts * depth, ff)
    rest, far = partials(got, largest, (held, weight), rows, experts, (3,), load=True)
    side, front = partials(got, largest, (held, rest), rows, experts, (1, 2))
    own, own_largest = partials(got, largest, (held, rest), rows, experts, (0,))
    near = [
        lax.ppermute(block, "expert", [(i, i ^ column) for i in range(n)])
        for column, block in ((1, side), (2, front), (3, far))
    ]
    planes = n // PLANE
    crossed = []
    for plane in range(1, planes):
        begin = plane * rows
        total = own[begin : begin + rows]
        top = own_largest[plane]
        for block in near:
            total += block[begin : begin + rows].astype(jnp.float32)
            top = jnp.maximum(top, block[planes * rows + plane, :LANES].astype(jnp.float32))
        merged = jnp.concatenate([total, jnp.broadcast_to(top, (rows, LANES))], axis=1)
        pairs = [(i, (i + plane * PLANE) % n) for i in range(n)]
        crossed.append(lax.ppermute(merged.astype(jnp.bfloat16), "expert", pairs))
    return finish(own, own_largest, near, crossed, rows)


def plain(tokens, routes, route_weights, learner_weights):
    n = lax.axis_size("expert")
    rows = tokens.shape[0]
    experts, depth, ff = learner_weights.shape
    largest = over_tensor(jnp.max(jnp.abs(learner_weights), axis=(1, 2)))
    chosen = routes[:, :, None] == jnp.arange(experts, dtype=jnp.int32)
    gate = jnp.sum(jnp.where(chosen, route_weights[:, :, None], 0.0), axis=1)
    high = lax.reduce_precision(gate, 8, 7)
    terms = jnp.concatenate([high, gate - high], axis=1).astype(jnp.bfloat16)
    columns = tokens.reshape(rows, n, depth).transpose(1, 0, 2)[::-1]
    top = jnp.broadcast_to(largest[::-1, None, None], (n, rows, 1))
    got = exchange(
        jnp.concatenate([columns, jnp.broadcast_to(terms, (n, *terms.shape)), top], axis=2), 1
    )
    weight = learner_weights.reshape(experts * depth, ff)

    def one(block):
        block = block.astype(jnp.float32)
        gates = block[:, depth : depth + experts] + block[:, depth + experts : depth + 2 * experts]
        scaled = (block[:, None, :depth] * gates[:, :, None]).astype(jnp.bfloat16)
        product = jnp.dot(
            scaled.reshape(rows, experts * depth), weight, preferred_element_type=jnp.float32
        )
        return product.astype(jnp.bfloat16)

    back = exchange(lax.map(one, got), 1)
    combined = jnp.sum(back.astype(jnp.float32), axis=0).astype(jnp.bfloat16)
    expert_amax = jnp.max(got[:, 0, depth + 2 * experts]).astype(jnp.float32).reshape(1)
    return (combined, expert_amax)


def shards(tokens, routes, route_weights, learner_weights):
    n, rows = lax.axis_size("expert"), tokens.shape[0]
    experts, depth, ff = learner_weights.shape
    aligned = depth % (2 * LANES) == 0 and ff % TILE == 0 and rows % 32 == 0 and n % PLANE == 0
    fits = lax.axis_size("tensor") == 2 and rows // SUBLANES * 2 * experts <= depth // 2
    small = experts * depth * ff <= 4 << 20 and n * rows <= 1024 and n <= PLANE * SUBLANES
    form = kernels if aligned and fits and small and experts == n else plain
    return form(tokens, routes, route_weights, learner_weights)


def solution(mesh):
    return jax.shard_map(
        shards,
        mesh=mesh,
        in_specs=(
            P("expert", None),
            P("expert", None),
            P("expert", None),
            P(None, "expert", "tensor"),
        ),
        out_specs=(P("expert", "tensor"), P("expert")),
        check_vma=False,
    )
```

```python
import functools

import jax
import jax.numpy as jnp
from jax import lax
from jax.experimental import pallas as pl
from jax.experimental.pallas import tpu as pltpu
from jax.sharding import PartitionSpec as P

LANES = 128
SUBLANES = 8
PLANE = 4
SENT = (1, 3)
VMEM = pl.BlockSpec(memory_space=pltpu.VMEM)
HBM = pl.BlockSpec(memory_space=pltpu.HBM)
TILE = 256


def flipped(index, n):
    return index ^ (n // 2 - 1)


def params(mebibytes):
    return pltpu.CompilerParams(vmem_limit_bytes=mebibytes << 20)


def pack_kernel(
    tokens_ref, routes_ref, weights_ref, send_ref, block_ref, routes_buf, weights_buf, sem, out_sem
):
    n, _, width = block_ref.shape
    choices, rows = routes_ref.shape
    core = lax.axis_index("tensor")
    copies = [
        pltpu.make_async_copy(routes_ref, routes_buf, sem.at[n]),
        pltpu.make_async_copy(weights_ref, weights_buf, sem.at[n + 1]),
    ]
    copies += [
        pltpu.make_async_copy(
            tokens_ref.at[:, pl.ds(pl.multiple_of((2 * flipped(i, n) + core) * width, LANES), width)],
            block_ref.at[i, pl.ds(0, rows)],
            sem.at[i],
        )
        for i in range(n)
    ]
    for copy in copies:
        copy.start()
    for copy in copies[:2]:
        copy.wait()
    expert = lax.broadcasted_iota(jnp.int32, (n, rows), 0)
    gate = jnp.zeros((n, rows), jnp.float32)
    for k in range(choices):
        chosen = routes_buf[k : k + 1, :] == expert
        gate += jnp.where(chosen, weights_buf[k : k + 1, :], 0.0)
    gate = gate.T
    high = gate.astype(jnp.bfloat16).astype(jnp.float32)
    low = gate - high
    terms = []
    for r in range(0, rows, SUBLANES):
        terms += [high[r : r + SUBLANES], low[r : r + SUBLANES]]
    spare = width - len(terms) * n
    if spare:
        terms.append(jnp.zeros((SUBLANES, spare), jnp.float32))
    packed = jnp.concatenate(terms, axis=1).astype(jnp.bfloat16)
    for i in range(n):
        block_ref[i, rows:, :] = packed
    group = n // 4
    outs = []
    for i in range(4):
        part = pl.ds(i * group, group)
        for copy in copies[2 + i * group : 2 + (i + 1) * group]:
            copy.wait()
        outs.append(pltpu.make_async_copy(block_ref.at[part], send_ref.at[part], out_sem.at[i]))
        outs[-1].start()
    for out in outs:
        out.wait()


def pack(tokens, routes, route_weights, n, width):
    rows, choices = routes.shape
    shape = (n, rows + SUBLANES, width)
    operands = (tokens, routes.T, route_weights.T)
    return pl.pallas_call(
        pack_kernel,
        out_shape=pltpu.HBM(shape, jnp.bfloat16),
        in_specs=[HBM] * 3,
        out_specs=HBM,
        scratch_shapes=[
            pltpu.VMEM(shape, jnp.bfloat16),
            pltpu.VMEM((choices, rows), jnp.int32),
            pltpu.VMEM((choices, rows), jnp.float32),
            pltpu.SemaphoreType.DMA((n + 2,)),
            pltpu.SemaphoreType.DMA((4,)),
        ],
        compiler_params=params(8),
    )(*(pltpu.with_memory_space_constraint(operand, pltpu.HBM) for operand in operands))


def largest_kernel(weight_ref, held_ref, largest_ref, rest_ref, sem):
    experts = weight_ref.shape[0]
    kept = held_ref.shape[0]
    places = [held_ref.at[e] if e < kept else rest_ref.at[e - kept] for e in range(experts)]
    copies = [
        pltpu.make_async_copy(weight_ref.at[e], place, sem.at[e]) for e, place in enumerate(places)
    ]
    for copy in copies:
        copy.start()
    for e, copy in enumerate(copies):
        copy.wait()
        block = jnp.abs(places[e][...].astype(jnp.float32))
        row = jnp.max(block, axis=0, keepdims=True)
        top = jnp.max(row, axis=1, keepdims=True)
        largest_ref[e : e + 1, :] = jnp.broadcast_to(top, (1, LANES))


def hold(weights):
    experts, depth, ff = weights.shape
    kept = experts // 2
    return pl.pallas_call(
        largest_kernel,
        out_shape=(
            pltpu.VMEM((kept, depth, ff), weights.dtype),
            jax.ShapeDtypeStruct((experts, LANES), jnp.float32),
        ),
        in_specs=[HBM],
        out_specs=(VMEM, VMEM),
        scratch_shapes=[
            pltpu.VMEM((experts - kept, depth, ff), weights.dtype),
            pltpu.SemaphoreType.DMA((experts,)),
        ],
        compiler_params=params(12),
        cost_estimate=pl.CostEstimate(
            flops=2 * weights.size, bytes_accessed=2 * weights.size, transcendentals=0
        ),
    )(pltpu.with_memory_space_constraint(weights, pltpu.HBM))


def place(role, plane):
    index, core = lax.axis_index("expert"), lax.axis_index("tensor")
    beyond = jnp.bitwise_xor(lax.div(index, PLANE), plane)
    away = {0: 0, 1: 1 + core, 2: 2 - core, 3: 3}[role]
    return beyond * PLANE + jnp.bitwise_xor(lax.rem(index, PLANE), away)


def partial_kernel(*refs, rows, experts, roles):
    kept_ref, swapped_ref, tail_ref, held_ref, rest_ref, *refs = refs
    *out_refs, scaled_ref, total_ref = refs
    n, _, width = kept_ref.shape
    ff, depth, planes = held_ref.shape[1], 2 * width, n // PLANE
    chips = [[place(role, plane) for plane in range(planes)] for role in roles]
    left = lax.axis_index("tensor") == 0
    deep = experts // 2 * depth
    blocks = []
    for role, column in zip(roles, chips):
        row = lax.broadcasted_iota(jnp.int32, (SUBLANES, LANES), 0)
        top = jnp.zeros((SUBLANES, LANES), jnp.float32)
        for plane, chip in enumerate(column):
            value = jnp.broadcast_to(tail_ref[pl.ds(chip, 1), :], (SUBLANES, LANES))
            top = jnp.where(row == plane, value, top)
        blocks.append(out_refs.pop(0))
        if role in SENT:
            blocks[-1][planes * rows :, :LANES] = top.astype(jnp.bfloat16)
            blocks[-1][planes * rows :, LANES:] = jnp.zeros(
                (SUBLANES, ff - LANES), jnp.bfloat16
            )
        else:
            out_refs.pop(0)[...] = top
    for i, chip in enumerate([chip for column in chips for chip in column]):
        at = flipped(chip, n)
        kept = kept_ref[at].astype(jnp.float32)
        swapped = swapped_ref[at, :rows].astype(jnp.float32)
        own = kept[:rows]
        x = jnp.concatenate([jnp.where(left, own, swapped), jnp.where(left, swapped, own)], axis=1)
        packed = kept[rows:]
        gates = jnp.concatenate(
            [
                packed[:, at : at + experts] + packed[:, at + experts : at + 2 * experts]
                for at in range(0, rows // SUBLANES * 2 * experts, 2 * experts)
            ],
            axis=0,
        )
        for e in range(experts):
            scaled_ref[i * rows : (i + 1) * rows, e * depth : (e + 1) * depth] = (
                x * gates[:, e : e + 1]
            ).astype(jnp.bfloat16)
    for i, part in enumerate((held_ref, rest_ref)):
        for at in range(0, ff, TILE):
            product = jnp.dot(
                scaled_ref[:, i * deep : (i + 1) * deep],
                part[:, at : at + TILE],
                preferred_element_type=jnp.float32,
            )
            if i == 0:
                total_ref[:, at : at + TILE] = product
                continue
            product += total_ref[:, at : at + TILE]
            for c, block in enumerate(blocks):
                block[: planes * rows, at : at + TILE] = product[
                    c * planes * rows : (c + 1) * planes * rows
                ].astype(block.dtype)


def partials(got, tail, weights, rows, experts, roles):
    n, _, width = got[0].shape
    depth, planes = 2 * width, n // PLANE
    deep, ff = weights[0].shape
    count = planes * rows * len(roles)
    held, rest = (pltpu.with_memory_space_constraint(part, pltpu.VMEM) for part in weights)
    out_shape = ()
    for role in roles:
        if role in SENT:
            out_shape += (jax.ShapeDtypeStruct((planes * rows + SUBLANES, ff), jnp.bfloat16),)
        else:
            out_shape += (
                jax.ShapeDtypeStruct((planes * rows, ff), jnp.float32),
                jax.ShapeDtypeStruct((SUBLANES, LANES), jnp.float32),
            )
    return pl.pallas_call(
        functools.partial(partial_kernel, rows=rows, experts=experts, roles=roles),
        out_shape=out_shape,
        in_specs=[VMEM] * 5,
        out_specs=(VMEM,) * len(out_shape),
        scratch_shapes=[
            pltpu.VMEM((count, experts * depth), jnp.bfloat16),
            pltpu.VMEM((count, ff), jnp.float32),
        ],
        compiler_params=params(16),
        cost_estimate=pl.CostEstimate(
            flops=2 * count * experts * depth * ff,
            bytes_accessed=4 * held.size,
            transcendentals=0,
        ),
    )(*got, tail, held, rest)


def finish_kernel(own_ref, largest_ref, *refs, planes):
    plane_refs, (*crossed_refs, out_ref, top_ref) = refs[:2], refs[2:]
    rows, ff = out_ref.shape
    total = own_ref[:rows]
    top = largest_ref[:1]
    for ref in plane_refs:
        total += ref[:rows].astype(jnp.float32)
        maxima = ref[planes * rows :, :LANES].astype(jnp.float32)
        top = jnp.maximum(top, maxima[:1])
    for ref in crossed_refs:
        total += ref[:, :ff].astype(jnp.float32)
        top = jnp.maximum(top, ref[:, ff:].astype(jnp.float32)[:1])
    out_ref[...] = total.astype(jnp.bfloat16)
    top_ref[0] = jnp.max(top)


def finish(own, largest, near, crossed, rows):
    operands = (own, largest, *near, *crossed)
    return pl.pallas_call(
        functools.partial(finish_kernel, planes=len(crossed) + 1),
        out_shape=(
            jax.ShapeDtypeStruct((rows, own.shape[1]), jnp.bfloat16),
            jax.ShapeDtypeStruct((1,), jnp.float32),
        ),
        in_specs=[VMEM] * len(operands),
        out_specs=(VMEM, pl.BlockSpec(memory_space=pltpu.SMEM)),
        compiler_params=params(8),
    )(*operands)


def exchange(block):
    n = lax.axis_size("expert")
    order = [flipped(i, n) for i in range(n)]
    return lax.all_to_all(
        block, "expert", split_axis=0, concat_axis=0, tiled=True, axis_index_groups=[order]
    )


def over_tensor(largest):
    if lax.axis_size("tensor") == 2:
        return jnp.maximum(largest, lax.ppermute(largest, "tensor", [(0, 1), (1, 0)]))
    return lax.pmax(largest, "tensor")


def kernels(tokens, routes, route_weights, learner_weights):
    n = lax.axis_size("expert")
    rows = tokens.shape[0]
    experts, depth, ff = learner_weights.shape
    got = exchange(pack(tokens, routes, route_weights, n, depth // 2))
    held, largest = hold(learner_weights)
    largest = over_tensor(largest)
    weight = learner_weights.reshape(experts * depth, ff)
    held = held.reshape(-1, ff)
    got, held, largest, weight = lax.optimization_barrier((got, held, largest, weight))
    got = (got, lax.ppermute(got, "tensor", [(0, 1), (1, 0)]))
    rest = weight[held.shape[0] :]
    (across,) = partials(got, largest, (held, rest), rows, experts, (3,))
    second, second_largest, first = partials(got, largest, (held, rest), rows, experts, (2, 1))
    own, own_largest = partials(got, largest, (held, rest), rows, experts, (0,))

    def over_link(block, step):
        links = [(1 + core, 2 - core)[step] for core in range(2)]
        pairs = [(2 * i + c, 2 * (i ^ links[c]) + c) for i in range(n) for c in range(2)]
        return lax.ppermute(block, ("expert", "tensor"), pairs)

    across = over_link(across, 0).astype(jnp.float32)
    end = n // PLANE * rows
    maxima = jnp.pad(second_largest, ((0, 0), (0, ff - LANES)))
    relay = jnp.concatenate([across[:end] + second, jnp.maximum(across[end:], maxima)])
    near = [over_link(relay.astype(jnp.bfloat16), 1), over_link(first, 0)]
    planes = n // PLANE
    crossed = []
    for plane in sorted(range(1, planes), key=lambda plane: (plane != 2, plane)):
        begin = plane * rows
        total = own[begin : begin + rows]
        top = own_largest[plane]
        for block in near:
            total += block[begin : begin + rows].astype(jnp.float32)
            top = jnp.maximum(top, block[planes * rows + plane, :LANES].astype(jnp.float32))
        merged = jnp.concatenate([total, jnp.broadcast_to(top, (rows, LANES))], axis=1)
        pairs = [(i, i ^ (plane * PLANE)) for i in range(n)]
        crossed.append(lax.ppermute(merged.astype(jnp.bfloat16), "expert", pairs))
    return finish(own, own_largest, near, crossed, rows)


def plain(tokens, routes, route_weights, learner_weights):
    n = lax.axis_size("expert")
    rows = tokens.shape[0]
    experts, depth, ff = learner_weights.shape
    largest = over_tensor(jnp.max(jnp.abs(learner_weights), axis=(1, 2)))
    chosen = routes[:, :, None] == jnp.arange(experts, dtype=jnp.int32)
    gate = jnp.sum(jnp.where(chosen, route_weights[:, :, None], 0.0), axis=1)
    high = lax.reduce_precision(gate, 8, 7)
    terms = jnp.concatenate([high, gate - high], axis=1).astype(jnp.bfloat16)
    columns = tokens.reshape(rows, n, depth).transpose(1, 0, 2)
    top = jnp.broadcast_to(largest[:, None, None], (n, rows, 1))
    got = jnp.concatenate([columns, jnp.broadcast_to(terms, (n, *terms.shape)), top], axis=2)
    got = lax.all_to_all(got, "expert", split_axis=0, concat_axis=0, tiled=True)
    weight = learner_weights.reshape(experts * depth, ff)

    def one(block):
        block = block.astype(jnp.float32)
        gates = block[:, depth : depth + experts] + block[:, depth + experts : depth + 2 * experts]
        scaled = (block[:, None, :depth] * gates[:, :, None]).astype(jnp.bfloat16)
        product = jnp.dot(
            scaled.reshape(rows, experts * depth), weight, preferred_element_type=jnp.float32
        )
        return product.astype(jnp.bfloat16)

    back = lax.map(one, got)
    back = lax.all_to_all(back, "expert", split_axis=0, concat_axis=0, tiled=True)
    combined = jnp.sum(back.astype(jnp.float32), axis=0).astype(jnp.bfloat16)
    expert_amax = jnp.max(got[:, 0, depth + 2 * experts]).astype(jnp.float32).reshape(1)
    return (combined, expert_amax)


def shards(tokens, routes, route_weights, learner_weights):
    n, rows = lax.axis_size("expert"), tokens.shape[0]
    experts, depth, ff = learner_weights.shape
    aligned = depth % (2 * LANES) == 0 and ff % TILE == 0 and rows % 32 == 0 and n in (8, 16, 32)
    fits = lax.axis_size("tensor") == 2 and rows // SUBLANES * 2 * experts <= depth // 2
    small = experts * depth * ff <= 4 << 20 and n * rows <= 1024 and n <= PLANE * SUBLANES
    form = kernels if aligned and fits and small and experts == n else plain
    return form(tokens, routes, route_weights, learner_weights)


def solution(mesh):
    return jax.shard_map(
        shards,
        mesh=mesh,
        in_specs=(
            P("expert", None),
            P("expert", None),
            P("expert", None),
            P(None, "expert", "tensor"),
        ),
        out_specs=(P("expert", "tensor"), P("expert")),
        check_vma=False,
    )
```

```python
import functools

import jax
import jax.numpy as jnp
from jax import lax
from jax.experimental import pallas as pl
from jax.experimental.pallas import tpu as pltpu
from jax.sharding import PartitionSpec as P

LANES = 128
SUBLANES = 8
PLANE = 4
SENT = (1, 3)
VMEM = pl.BlockSpec(memory_space=pltpu.VMEM)
HBM = pl.BlockSpec(memory_space=pltpu.HBM)
TILE = 256


def flipped(index, n):
    return index ^ (n // 2 - 1)


def params(mebibytes):
    return pltpu.CompilerParams(vmem_limit_bytes=mebibytes << 20)


def pack_kernel(
    tokens_ref, routes_ref, weights_ref, send_ref, block_ref, routes_buf, weights_buf, sem, out_sem
):
    n, _, width = block_ref.shape
    choices, rows = routes_ref.shape
    core = lax.axis_index("tensor")
    copies = [
        pltpu.make_async_copy(routes_ref, routes_buf, sem.at[n]),
        pltpu.make_async_copy(weights_ref, weights_buf, sem.at[n + 1]),
    ]
    copies += [
        pltpu.make_async_copy(
            tokens_ref.at[:, pl.ds(pl.multiple_of((2 * flipped(i, n) + core) * width, LANES), width)],
            block_ref.at[i, pl.ds(0, rows)],
            sem.at[i],
        )
        for i in range(n)
    ]
    for copy in copies:
        copy.start()
    for copy in copies[:2]:
        copy.wait()
    expert = lax.broadcasted_iota(jnp.int32, (n, rows), 0)
    gate = jnp.zeros((n, rows), jnp.float32)
    for k in range(choices):
        chosen = routes_buf[k : k + 1, :] == expert
        gate += jnp.where(chosen, weights_buf[k : k + 1, :], 0.0)
    gate = gate.T
    high = gate.astype(jnp.bfloat16).astype(jnp.float32)
    low = gate - high
    terms = []
    for r in range(0, rows, SUBLANES):
        terms += [high[r : r + SUBLANES], low[r : r + SUBLANES]]
    spare = width - len(terms) * n
    if spare:
        terms.append(jnp.zeros((SUBLANES, spare), jnp.float32))
    packed = jnp.concatenate(terms, axis=1).astype(jnp.bfloat16)
    for i in range(n):
        block_ref[i, rows:, :] = packed
    group = n // 4
    outs = []
    for i in range(4):
        part = pl.ds(i * group, group)
        for copy in copies[2 + i * group : 2 + (i + 1) * group]:
            copy.wait()
        outs.append(pltpu.make_async_copy(block_ref.at[part], send_ref.at[part], out_sem.at[i]))
        outs[-1].start()
    for out in outs:
        out.wait()


def pack(tokens, routes, route_weights, n, width):
    rows, choices = routes.shape
    shape = (n, rows + SUBLANES, width)
    operands = (tokens, routes.T, route_weights.T)
    return pl.pallas_call(
        pack_kernel,
        out_shape=pltpu.HBM(shape, jnp.bfloat16),
        in_specs=[HBM] * 3,
        out_specs=HBM,
        scratch_shapes=[
            pltpu.VMEM(shape, jnp.bfloat16),
            pltpu.VMEM((choices, rows), jnp.int32),
            pltpu.VMEM((choices, rows), jnp.float32),
            pltpu.SemaphoreType.DMA((n + 2,)),
            pltpu.SemaphoreType.DMA((4,)),
        ],
        compiler_params=params(8),
    )(*(pltpu.with_memory_space_constraint(operand, pltpu.HBM) for operand in operands))


def largest_kernel(weight_ref, held_ref, largest_ref, rest_ref, sem):
    experts = weight_ref.shape[0]
    kept = held_ref.shape[0]
    places = [held_ref.at[e] if e < kept else rest_ref.at[e - kept] for e in range(experts)]
    copies = [
        pltpu.make_async_copy(weight_ref.at[e], place, sem.at[e]) for e, place in enumerate(places)
    ]
    for copy in copies:
        copy.start()
    for e, copy in enumerate(copies):
        copy.wait()
        block = jnp.abs(places[e][...].astype(jnp.float32))
        row = jnp.max(block, axis=0, keepdims=True)
        top = jnp.max(row, axis=1, keepdims=True)
        largest_ref[e : e + 1, :] = jnp.broadcast_to(top, (1, LANES))


def hold(weights):
    experts, depth, ff = weights.shape
    kept = experts // 2
    return pl.pallas_call(
        largest_kernel,
        out_shape=(
            pltpu.VMEM((kept, depth, ff), weights.dtype),
            jax.ShapeDtypeStruct((experts, LANES), jnp.float32),
        ),
        in_specs=[HBM],
        out_specs=(VMEM, VMEM),
        scratch_shapes=[
            pltpu.VMEM((experts - kept, depth, ff), weights.dtype),
            pltpu.SemaphoreType.DMA((experts,)),
        ],
        compiler_params=params(12),
        cost_estimate=pl.CostEstimate(
            flops=2 * weights.size, bytes_accessed=2 * weights.size, transcendentals=0
        ),
    )(pltpu.with_memory_space_constraint(weights, pltpu.HBM))


def place(role, plane):
    index, core = lax.axis_index("expert"), lax.axis_index("tensor")
    beyond = jnp.bitwise_xor(lax.div(index, PLANE), plane)
    away = {0: 0, 1: 1 + core, 2: 2 - core, 3: 3}[role]
    return beyond * PLANE + jnp.bitwise_xor(lax.rem(index, PLANE), away)


def partial_kernel(*refs, rows, experts, roles):
    kept_ref, swapped_ref, tail_ref, held_ref, rest_ref, *refs = refs
    *out_refs, scaled_ref, total_ref = refs
    n, _, width = kept_ref.shape
    ff, depth, planes = held_ref.shape[1], 2 * width, n // PLANE
    chips = [[place(role, plane) for plane in range(planes)] for role in roles]
    left = lax.axis_index("tensor") == 0
    deep = experts // 2 * depth
    blocks = []
    for role, column in zip(roles, chips):
        row = lax.broadcasted_iota(jnp.int32, (SUBLANES, LANES), 0)
        top = jnp.zeros((SUBLANES, LANES), jnp.float32)
        for plane, chip in enumerate(column):
            value = jnp.broadcast_to(tail_ref[pl.ds(chip, 1), :], (SUBLANES, LANES))
            top = jnp.where(row == plane, value, top)
        blocks.append(out_refs.pop(0))
        if role in SENT:
            blocks[-1][planes * rows :, :LANES] = top.astype(jnp.bfloat16)
            blocks[-1][planes * rows :, LANES:] = jnp.zeros(
                (SUBLANES, ff - LANES), jnp.bfloat16
            )
        else:
            out_refs.pop(0)[...] = top
    for i, chip in enumerate([chip for column in chips for chip in column]):
        at = flipped(chip, n)
        kept = kept_ref[at].astype(jnp.float32)
        swapped = swapped_ref[at, :rows].astype(jnp.float32)
        own = kept[:rows]
        x = jnp.concatenate([jnp.where(left, own, swapped), jnp.where(left, swapped, own)], axis=1)
        packed = kept[rows:]
        gates = jnp.concatenate(
            [
                packed[:, at : at + experts] + packed[:, at + experts : at + 2 * experts]
                for at in range(0, rows // SUBLANES * 2 * experts, 2 * experts)
            ],
            axis=0,
        )
        for e in range(experts):
            scaled_ref[i * rows : (i + 1) * rows, e * depth : (e + 1) * depth] = (
                x * gates[:, e : e + 1]
            ).astype(jnp.bfloat16)
    for i, part in enumerate((held_ref, rest_ref)):
        for at in range(0, ff, TILE):
            product = jnp.dot(
                scaled_ref[:, i * deep : (i + 1) * deep],
                part[:, at : at + TILE],
                preferred_element_type=jnp.float32,
            )
            if i == 0:
                total_ref[:, at : at + TILE] = product
                continue
            product += total_ref[:, at : at + TILE]
            for c, block in enumerate(blocks):
                block[: planes * rows, at : at + TILE] = product[
                    c * planes * rows : (c + 1) * planes * rows
                ].astype(block.dtype)


def partials(got, tail, weights, rows, experts, roles):
    n, _, width = got[0].shape
    depth, planes = 2 * width, n // PLANE
    deep, ff = weights[0].shape
    count = planes * rows * len(roles)
    held, rest = (pltpu.with_memory_space_constraint(part, pltpu.VMEM) for part in weights)
    out_shape = ()
    for role in roles:
        if role in SENT:
            out_shape += (jax.ShapeDtypeStruct((planes * rows + SUBLANES, ff), jnp.bfloat16),)
        else:
            out_shape += (
                jax.ShapeDtypeStruct((planes * rows, ff), jnp.float32),
                jax.ShapeDtypeStruct((SUBLANES, LANES), jnp.float32),
            )
    return pl.pallas_call(
        functools.partial(partial_kernel, rows=rows, experts=experts, roles=roles),
        out_shape=out_shape,
        in_specs=[VMEM] * 5,
        out_specs=(VMEM,) * len(out_shape),
        scratch_shapes=[
            pltpu.VMEM((count, experts * depth), jnp.bfloat16),
            pltpu.VMEM((count, ff), jnp.float32),
        ],
        compiler_params=params(16),
        cost_estimate=pl.CostEstimate(
            flops=2 * count * experts * depth * ff,
            bytes_accessed=4 * held.size,
            transcendentals=0,
        ),
    )(*got, tail, held, rest)


def finish_kernel(own_ref, largest_ref, *refs, planes):
    plane_refs, (*crossed_refs, out_ref, top_ref) = refs[:2], refs[2:]
    rows, ff = out_ref.shape
    total = own_ref[:rows]
    top = largest_ref[:1]
    for ref in plane_refs:
        total += ref[:rows].astype(jnp.float32)
        maxima = ref[planes * rows :, :LANES].astype(jnp.float32)
        top = jnp.maximum(top, maxima[:1])
    wide, tall = ff // LANES, rows // SUBLANES
    tiles = [jnp.zeros((SUBLANES, LANES), jnp.float32)] * (wide * tall)
    for ref in crossed_refs:
        tiles = [tile + ref[i].astype(jnp.float32) for i, tile in enumerate(tiles)]
        top = jnp.maximum(top, ref[wide * tall].astype(jnp.float32)[:1])
    crossed = [jnp.concatenate(tiles[i * wide : (i + 1) * wide], axis=1) for i in range(tall)]
    out_ref[...] = (total + jnp.concatenate(crossed)).astype(jnp.bfloat16)
    top_ref[0] = jnp.max(top)


def finish(own, largest, near, crossed, rows):
    operands = (own, largest, *near, *crossed)
    return pl.pallas_call(
        functools.partial(finish_kernel, planes=len(crossed) + 1),
        out_shape=(
            jax.ShapeDtypeStruct((rows, own.shape[1]), jnp.bfloat16),
            jax.ShapeDtypeStruct((1,), jnp.float32),
        ),
        in_specs=[VMEM] * len(operands),
        out_specs=(VMEM, pl.BlockSpec(memory_space=pltpu.SMEM)),
        compiler_params=params(8),
    )(*operands)


def exchange(block):
    n = lax.axis_size("expert")
    order = [flipped(i, n) for i in range(n)]
    return lax.all_to_all(
        block, "expert", split_axis=0, concat_axis=0, tiled=True, axis_index_groups=[order]
    )


def over_tensor(largest):
    if lax.axis_size("tensor") == 2:
        return jnp.maximum(largest, lax.ppermute(largest, "tensor", [(0, 1), (1, 0)]))
    return lax.pmax(largest, "tensor")


def kernels(tokens, routes, route_weights, learner_weights):
    n = lax.axis_size("expert")
    rows = tokens.shape[0]
    experts, depth, ff = learner_weights.shape
    got = exchange(pack(tokens, routes, route_weights, n, depth // 2))
    held, largest = hold(learner_weights)
    largest = over_tensor(largest)
    weight = learner_weights.reshape(experts * depth, ff)
    held = held.reshape(-1, ff)
    got, held, largest, weight = lax.optimization_barrier((got, held, largest, weight))
    got = (got, lax.ppermute(got, "tensor", [(0, 1), (1, 0)]))
    rest = weight[held.shape[0] :]
    (across,) = partials(got, largest, (held, rest), rows, experts, (3,))
    second, second_largest, first = partials(got, largest, (held, rest), rows, experts, (2, 1))
    own, own_largest = partials(got, largest, (held, rest), rows, experts, (0,))

    def over_link(block, step):
        links = [(1 + core, 2 - core)[step] for core in range(2)]
        pairs = [(2 * i + c, 2 * (i ^ links[c]) + c) for i in range(n) for c in range(2)]
        return lax.ppermute(block, ("expert", "tensor"), pairs)

    across = over_link(across, 0).astype(jnp.float32)
    end = n // PLANE * rows
    maxima = jnp.pad(second_largest, ((0, 0), (0, ff - LANES)))
    relay = jnp.concatenate([across[:end] + second, jnp.maximum(across[end:], maxima)])
    near = [over_link(relay.astype(jnp.bfloat16), 1), over_link(first, 0)]
    planes = n // PLANE
    crossed = []
    for plane in sorted(range(1, planes), key=lambda plane: (plane != 2, plane)):
        begin = plane * rows
        total = own[begin : begin + rows]
        top = own_largest[plane]
        for block in near:
            total += block[begin : begin + rows].astype(jnp.float32)
            top = jnp.maximum(top, block[planes * rows + plane, :LANES].astype(jnp.float32))
        tiles = total.reshape(rows // SUBLANES, SUBLANES, ff // LANES, LANES)
        tiles = tiles.transpose(0, 2, 1, 3).reshape(-1, SUBLANES, LANES)
        merged = jnp.concatenate([tiles, jnp.broadcast_to(top, (1, SUBLANES, LANES))])
        pairs = [(i, i ^ (plane * PLANE)) for i in range(n)]
        crossed.append(lax.ppermute(merged.astype(jnp.bfloat16), "expert", pairs))
    return finish(own, own_largest, near, crossed, rows)


def plain(tokens, routes, route_weights, learner_weights):
    n = lax.axis_size("expert")
    rows = tokens.shape[0]
    experts, depth, ff = learner_weights.shape
    largest = over_tensor(jnp.max(jnp.abs(learner_weights), axis=(1, 2)))
    chosen = routes[:, :, None] == jnp.arange(experts, dtype=jnp.int32)
    gate = jnp.sum(jnp.where(chosen, route_weights[:, :, None], 0.0), axis=1)
    high = lax.reduce_precision(gate, 8, 7)
    terms = jnp.concatenate([high, gate - high], axis=1).astype(jnp.bfloat16)
    columns = tokens.reshape(rows, n, depth).transpose(1, 0, 2)
    top = jnp.broadcast_to(largest[:, None, None], (n, rows, 1))
    got = jnp.concatenate([columns, jnp.broadcast_to(terms, (n, *terms.shape)), top], axis=2)
    got = lax.all_to_all(got, "expert", split_axis=0, concat_axis=0, tiled=True)
    weight = learner_weights.reshape(experts * depth, ff)

    def one(block):
        block = block.astype(jnp.float32)
        gates = block[:, depth : depth + experts] + block[:, depth + experts : depth + 2 * experts]
        scaled = (block[:, None, :depth] * gates[:, :, None]).astype(jnp.bfloat16)
        product = jnp.dot(
            scaled.reshape(rows, experts * depth), weight, preferred_element_type=jnp.float32
        )
        return product.astype(jnp.bfloat16)

    back = lax.map(one, got)
    back = lax.all_to_all(back, "expert", split_axis=0, concat_axis=0, tiled=True)
    combined = jnp.sum(back.astype(jnp.float32), axis=0).astype(jnp.bfloat16)
    expert_amax = jnp.max(got[:, 0, depth + 2 * experts]).astype(jnp.float32).reshape(1)
    return (combined, expert_amax)


def shards(tokens, routes, route_weights, learner_weights):
    n, rows = lax.axis_size("expert"), tokens.shape[0]
    experts, depth, ff = learner_weights.shape
    aligned = depth % (2 * LANES) == 0 and ff % TILE == 0 and rows % 32 == 0 and n in (8, 16, 32)
    fits = lax.axis_size("tensor") == 2 and rows // SUBLANES * 2 * experts <= depth // 2
    small = experts * depth * ff <= 4 << 20 and n * rows <= 1024 and n <= PLANE * SUBLANES
    form = kernels if aligned and fits and small and experts == n else plain
    return form(tokens, routes, route_weights, learner_weights)


def solution(mesh):
    return jax.shard_map(
        shards,
        mesh=mesh,
        in_specs=(
            P("expert", None),
            P("expert", None),
            P("expert", None),
            P(None, "expert", "tensor"),
        ),
        out_specs=(P("expert", "tensor"), P("expert")),
        check_vma=False,
    )
```

```python
import functools

import jax
import jax.numpy as jnp
from jax import lax
from jax.experimental import pallas as pl
from jax.experimental.pallas import tpu as pltpu
from jax.sharding import PartitionSpec as P

LANES = 128
SUBLANES = 8
PLANE = 4
SENT = (1, 3)
VMEM = pl.BlockSpec(memory_space=pltpu.VMEM)
HBM = pl.BlockSpec(memory_space=pltpu.HBM)
TILE = 256


def flipped(index, n):
    return index ^ (n // 2 - 1)


def params(mebibytes):
    return pltpu.CompilerParams(vmem_limit_bytes=mebibytes << 20)


def pack_kernel(
    tokens_ref, routes_ref, weights_ref, send_ref, block_ref, routes_buf, weights_buf, sem, out_sem
):
    n, _, width = block_ref.shape
    choices, rows = routes_ref.shape
    core = lax.axis_index("tensor")
    copies = [
        pltpu.make_async_copy(routes_ref, routes_buf, sem.at[n]),
        pltpu.make_async_copy(weights_ref, weights_buf, sem.at[n + 1]),
    ]
    copies += [
        pltpu.make_async_copy(
            tokens_ref.at[:, pl.ds(pl.multiple_of((2 * flipped(i, n) + core) * width, LANES), width)],
            block_ref.at[i, pl.ds(0, rows)],
            sem.at[i],
        )
        for i in range(n)
    ]
    for copy in copies:
        copy.start()
    for copy in copies[:2]:
        copy.wait()
    expert = lax.broadcasted_iota(jnp.int32, (n, rows), 0)
    gate = jnp.zeros((n, rows), jnp.float32)
    for k in range(choices):
        chosen = routes_buf[k : k + 1, :] == expert
        gate += jnp.where(chosen, weights_buf[k : k + 1, :], 0.0)
    gate = gate.T
    high = gate.astype(jnp.bfloat16).astype(jnp.float32)
    low = gate - high
    terms = []
    for r in range(0, rows, SUBLANES):
        terms += [high[r : r + SUBLANES], low[r : r + SUBLANES]]
    spare = width - len(terms) * n
    if spare:
        terms.append(jnp.zeros((SUBLANES, spare), jnp.float32))
    packed = jnp.concatenate(terms, axis=1).astype(jnp.bfloat16)
    for i in range(n):
        block_ref[i, rows:, :] = packed
    group = n // 4
    outs = []
    for i in range(4):
        part = pl.ds(i * group, group)
        for copy in copies[2 + i * group : 2 + (i + 1) * group]:
            copy.wait()
        outs.append(pltpu.make_async_copy(block_ref.at[part], send_ref.at[part], out_sem.at[i]))
        outs[-1].start()
    for out in outs:
        out.wait()


def pack(tokens, routes, route_weights, n, width):
    rows, choices = routes.shape
    shape = (n, rows + SUBLANES, width)
    operands = (tokens, routes.T, route_weights.T)
    return pl.pallas_call(
        pack_kernel,
        out_shape=pltpu.HBM(shape, jnp.bfloat16),
        in_specs=[HBM] * 3,
        out_specs=HBM,
        scratch_shapes=[
            pltpu.VMEM(shape, jnp.bfloat16),
            pltpu.VMEM((choices, rows), jnp.int32),
            pltpu.VMEM((choices, rows), jnp.float32),
            pltpu.SemaphoreType.DMA((n + 2,)),
            pltpu.SemaphoreType.DMA((4,)),
        ],
        compiler_params=params(8),
    )(*(pltpu.with_memory_space_constraint(operand, pltpu.HBM) for operand in operands))


def largest_kernel(weight_ref, held_ref, largest_ref, rest_ref, sem):
    experts = weight_ref.shape[0]
    kept = held_ref.shape[0]
    places = [held_ref.at[e] if e < kept else rest_ref.at[e - kept] for e in range(experts)]
    copies = [
        pltpu.make_async_copy(weight_ref.at[e], place, sem.at[e]) for e, place in enumerate(places)
    ]
    for copy in copies:
        copy.start()
    for e, copy in enumerate(copies):
        copy.wait()
        block = jnp.abs(places[e][...].astype(jnp.float32))
        row = jnp.max(block, axis=0, keepdims=True)
        top = jnp.max(row, axis=1, keepdims=True)
        largest_ref[e : e + 1, :] = jnp.broadcast_to(top, (1, LANES))


def hold(weights):
    experts, depth, ff = weights.shape
    kept = experts // 2
    return pl.pallas_call(
        largest_kernel,
        out_shape=(
            pltpu.VMEM((kept, depth, ff), weights.dtype),
            jax.ShapeDtypeStruct((experts, LANES), jnp.float32),
        ),
        in_specs=[HBM],
        out_specs=(VMEM, VMEM),
        scratch_shapes=[
            pltpu.VMEM((experts - kept, depth, ff), weights.dtype),
            pltpu.SemaphoreType.DMA((experts,)),
        ],
        compiler_params=params(12),
        cost_estimate=pl.CostEstimate(
            flops=2 * weights.size, bytes_accessed=2 * weights.size, transcendentals=0
        ),
    )(pltpu.with_memory_space_constraint(weights, pltpu.HBM))


def place(role, plane):
    index, core = lax.axis_index("expert"), lax.axis_index("tensor")
    beyond = jnp.bitwise_xor(lax.div(index, PLANE), plane)
    away = {0: 0, 1: 1 + core, 2: 2 - core, 3: 3}[role]
    return beyond * PLANE + jnp.bitwise_xor(lax.rem(index, PLANE), away)


def partial_kernel(*refs, rows, experts, roles):
    kept_ref, swapped_ref, tail_ref, held_ref, rest_ref, *refs = refs
    *out_refs, scaled_ref, total_ref = refs
    n, _, width = kept_ref.shape
    ff, depth, planes = held_ref.shape[1], 2 * width, n // PLANE
    chips = [[place(role, plane) for plane in range(planes)] for role in roles]
    left = lax.axis_index("tensor") == 0
    deep = experts // 2 * depth
    blocks = []
    for role, column in zip(roles, chips):
        row = lax.broadcasted_iota(jnp.int32, (SUBLANES, LANES), 0)
        top = jnp.zeros((SUBLANES, LANES), jnp.float32)
        for plane, chip in enumerate(column):
            value = jnp.broadcast_to(tail_ref[pl.ds(chip, 1), :], (SUBLANES, LANES))
            top = jnp.where(row == plane, value, top)
        blocks.append(out_refs.pop(0))
        if role in SENT:
            blocks[-1][blocks[-1].shape[0] - 1] = top.astype(jnp.bfloat16)
        else:
            out_refs.pop(0)[...] = top
    for i, chip in enumerate([chip for column in chips for chip in column]):
        at = flipped(chip, n)
        kept = kept_ref[at].astype(jnp.float32)
        swapped = swapped_ref[at, :rows].astype(jnp.float32)
        own = kept[:rows]
        x = jnp.concatenate([jnp.where(left, own, swapped), jnp.where(left, swapped, own)], axis=1)
        packed = kept[rows:]
        gates = jnp.concatenate(
            [
                packed[:, at : at + experts] + packed[:, at + experts : at + 2 * experts]
                for at in range(0, rows // SUBLANES * 2 * experts, 2 * experts)
            ],
            axis=0,
        )
        for e in range(experts):
            scaled_ref[i * rows : (i + 1) * rows, e * depth : (e + 1) * depth] = (
                x * gates[:, e : e + 1]
            ).astype(jnp.bfloat16)
    for i, part in enumerate((held_ref, rest_ref)):
        for at in range(0, ff, TILE):
            product = jnp.dot(
                scaled_ref[:, i * deep : (i + 1) * deep],
                part[:, at : at + TILE],
                preferred_element_type=jnp.float32,
            )
            if i == 0:
                total_ref[:, at : at + TILE] = product
                continue
            product += total_ref[:, at : at + TILE]
            for c, (role, block) in enumerate(zip(roles, blocks)):
                piece = product[c * planes * rows : (c + 1) * planes * rows]
                if role not in SENT:
                    block[:, at : at + TILE] = piece
                    continue
                for r in range(planes * rows // SUBLANES):
                    for lane in range(0, TILE, LANES):
                        block[r * (ff // LANES) + (at + lane) // LANES] = piece[
                            r * SUBLANES : (r + 1) * SUBLANES, lane : lane + LANES
                        ].astype(block.dtype)


def partials(got, tail, weights, rows, experts, roles):
    n, _, width = got[0].shape
    depth, planes = 2 * width, n // PLANE
    deep, ff = weights[0].shape
    count = planes * rows * len(roles)
    held, rest = (pltpu.with_memory_space_constraint(part, pltpu.VMEM) for part in weights)
    out_shape = ()
    for role in roles:
        if role in SENT:
            tiles = planes * rows * ff // (SUBLANES * LANES) + 1
            out_shape += (jax.ShapeDtypeStruct((tiles, SUBLANES, LANES), jnp.bfloat16),)
        else:
            out_shape += (
                jax.ShapeDtypeStruct((planes * rows, ff), jnp.float32),
                jax.ShapeDtypeStruct((SUBLANES, LANES), jnp.float32),
            )
    return pl.pallas_call(
        functools.partial(partial_kernel, rows=rows, experts=experts, roles=roles),
        out_shape=out_shape,
        in_specs=[VMEM] * 5,
        out_specs=(VMEM,) * len(out_shape),
        scratch_shapes=[
            pltpu.VMEM((count, experts * depth), jnp.bfloat16),
            pltpu.VMEM((count, ff), jnp.float32),
        ],
        compiler_params=params(16),
        cost_estimate=pl.CostEstimate(
            flops=2 * count * experts * depth * ff,
            bytes_accessed=4 * held.size,
            transcendentals=0,
        ),
    )(*got, tail, held, rest)


def finish_kernel(own_ref, largest_ref, *refs):
    plane_refs, (*crossed_refs, out_ref, top_ref) = refs[:2], refs[2:]
    rows, ff = out_ref.shape
    wide, tall = ff // LANES, rows // SUBLANES
    top = largest_ref[:1]
    tiles = [jnp.zeros((SUBLANES, LANES), jnp.float32)] * (wide * tall)
    for ref in (*plane_refs, *crossed_refs):
        tiles = [tile + ref[i].astype(jnp.float32) for i, tile in enumerate(tiles)]
        top = jnp.maximum(top, ref[ref.shape[0] - 1].astype(jnp.float32)[:1])
    total = [jnp.concatenate(tiles[i * wide : (i + 1) * wide], axis=1) for i in range(tall)]
    out_ref[...] = (own_ref[:rows] + jnp.concatenate(total)).astype(jnp.bfloat16)
    top_ref[0] = jnp.max(top)


def finish(own, largest, near, crossed, rows):
    operands = (own, largest, *near, *crossed)
    return pl.pallas_call(
        finish_kernel,
        out_shape=(
            jax.ShapeDtypeStruct((rows, own.shape[1]), jnp.bfloat16),
            jax.ShapeDtypeStruct((1,), jnp.float32),
        ),
        in_specs=[VMEM] * len(operands),
        out_specs=(VMEM, pl.BlockSpec(memory_space=pltpu.SMEM)),
        compiler_params=params(8),
    )(*operands)


def exchange(block):
    n = lax.axis_size("expert")
    order = [flipped(i, n) for i in range(n)]
    return lax.all_to_all(
        block, "expert", split_axis=0, concat_axis=0, tiled=True, axis_index_groups=[order]
    )


def over_tensor(largest):
    if lax.axis_size("tensor") == 2:
        return jnp.maximum(largest, lax.ppermute(largest, "tensor", [(0, 1), (1, 0)]))
    return lax.pmax(largest, "tensor")


def kernels(tokens, routes, route_weights, learner_weights):
    n = lax.axis_size("expert")
    rows = tokens.shape[0]
    experts, depth, ff = learner_weights.shape
    got = exchange(pack(tokens, routes, route_weights, n, depth // 2))
    held, largest = hold(learner_weights)
    largest = over_tensor(largest)
    weight = learner_weights.reshape(experts * depth, ff)
    held = held.reshape(-1, ff)
    got, held, largest, weight = lax.optimization_barrier((got, held, largest, weight))
    got = (got, lax.ppermute(got, "tensor", [(0, 1), (1, 0)]))
    rest = weight[held.shape[0] :]
    (across,) = partials(got, largest, (held, rest), rows, experts, (3,))
    second, second_largest, first = partials(got, largest, (held, rest), rows, experts, (2, 1))
    own, own_largest = partials(got, largest, (held, rest), rows, experts, (0,))

    def over_link(block, step):
        links = [(1 + core, 2 - core)[step] for core in range(2)]
        pairs = [(2 * i + c, 2 * (i ^ links[c]) + c) for i in range(n) for c in range(2)]
        return lax.ppermute(block, ("expert", "tensor"), pairs)

    def tiles_of(block):
        tiles = block.reshape(-1, SUBLANES, ff // LANES, LANES)
        return tiles.transpose(0, 2, 1, 3).reshape(-1, SUBLANES, LANES)

    across = over_link(across, 0).astype(jnp.float32)
    relay = jnp.concatenate(
        [across[:-1] + tiles_of(second), jnp.maximum(across[-1:], second_largest[None])]
    )
    near = [over_link(relay.astype(jnp.bfloat16), 1), over_link(first, 0)]
    planes = n // PLANE
    size = rows * ff // (SUBLANES * LANES)
    own_tiles = tiles_of(own)
    crossed = []
    for plane in sorted(range(1, planes), key=lambda plane: (plane != 2, plane)):
        total = own_tiles[plane * size : (plane + 1) * size]
        top = own_largest[plane]
        for block in near:
            total += block[plane * size : (plane + 1) * size].astype(jnp.float32)
            top = jnp.maximum(top, block[-1, plane].astype(jnp.float32))
        merged = jnp.concatenate([total, jnp.broadcast_to(top, (1, SUBLANES, LANES))])
        pairs = [(i, i ^ (plane * PLANE)) for i in range(n)]
        crossed.append(lax.ppermute(merged.astype(jnp.bfloat16), "expert", pairs))
    return finish(own, own_largest, near, crossed, rows)


def plain(tokens, routes, route_weights, learner_weights):
    n = lax.axis_size("expert")
    rows = tokens.shape[0]
    experts, depth, ff = learner_weights.shape
    largest = over_tensor(jnp.max(jnp.abs(learner_weights), axis=(1, 2)))
    chosen = routes[:, :, None] == jnp.arange(experts, dtype=jnp.int32)
    gate = jnp.sum(jnp.where(chosen, route_weights[:, :, None], 0.0), axis=1)
    high = lax.reduce_precision(gate, 8, 7)
    terms = jnp.concatenate([high, gate - high], axis=1).astype(jnp.bfloat16)
    columns = tokens.reshape(rows, n, depth).transpose(1, 0, 2)
    top = jnp.broadcast_to(largest[:, None, None], (n, rows, 1))
    got = jnp.concatenate([columns, jnp.broadcast_to(terms, (n, *terms.shape)), top], axis=2)
    got = lax.all_to_all(got, "expert", split_axis=0, concat_axis=0, tiled=True)
    weight = learner_weights.reshape(experts * depth, ff)

    def one(block):
        block = block.astype(jnp.float32)
        gates = block[:, depth : depth + experts] + block[:, depth + experts : depth + 2 * experts]
        scaled = (block[:, None, :depth] * gates[:, :, None]).astype(jnp.bfloat16)
        product = jnp.dot(
            scaled.reshape(rows, experts * depth), weight, preferred_element_type=jnp.float32
        )
        return product.astype(jnp.bfloat16)

    back = lax.map(one, got)
    back = lax.all_to_all(back, "expert", split_axis=0, concat_axis=0, tiled=True)
    combined = jnp.sum(back.astype(jnp.float32), axis=0).astype(jnp.bfloat16)
    expert_amax = jnp.max(got[:, 0, depth + 2 * experts]).astype(jnp.float32).reshape(1)
    return (combined, expert_amax)


def shards(tokens, routes, route_weights, learner_weights):
    n, rows = lax.axis_size("expert"), tokens.shape[0]
    experts, depth, ff = learner_weights.shape
    aligned = depth % (2 * LANES) == 0 and ff % TILE == 0 and rows % 32 == 0 and n in (8, 16, 32)
    fits = lax.axis_size("tensor") == 2 and rows // SUBLANES * 2 * experts <= depth // 2
    small = experts * depth * ff <= 4 << 20 and n * rows <= 1024 and n <= PLANE * SUBLANES
    form = kernels if aligned and fits and small and experts == n else plain
    return form(tokens, routes, route_weights, learner_weights)


def solution(mesh):
    return jax.shard_map(
        shards,
        mesh=mesh,
        in_specs=(
            P("expert", None),
            P("expert", None),
            P("expert", None),
            P(None, "expert", "tensor"),
        ),
        out_specs=(P("expert", "tensor"), P("expert")),
        check_vma=False,
    )
```

```python
import functools

import jax
import jax.numpy as jnp
from jax import lax
from jax.experimental import pallas as pl
from jax.experimental.pallas import tpu as pltpu
from jax.sharding import PartitionSpec as P

LANES = 128
SUBLANES = 8
PLANE = 4
SENT = (1, 3)
VMEM = pl.BlockSpec(memory_space=pltpu.VMEM)
HBM = pl.BlockSpec(memory_space=pltpu.HBM)
TILE = 256


def flipped(index, n):
    return index ^ (n // 2 - 1)


def params(mebibytes):
    return pltpu.CompilerParams(vmem_limit_bytes=mebibytes << 20)


def pack_kernel(
    tokens_ref, routes_ref, weights_ref, send_ref, block_ref, routes_buf, weights_buf, sem, out_sem
):
    n, _, width = block_ref.shape
    choices, rows = routes_ref.shape
    core = lax.axis_index("tensor")
    copies = [
        pltpu.make_async_copy(routes_ref, routes_buf, sem.at[n]),
        pltpu.make_async_copy(weights_ref, weights_buf, sem.at[n + 1]),
    ]
    copies += [
        pltpu.make_async_copy(
            tokens_ref.at[:, pl.ds(pl.multiple_of((2 * flipped(i, n) + core) * width, LANES), width)],
            block_ref.at[i, pl.ds(0, rows)],
            sem.at[i],
        )
        for i in range(n)
    ]
    for copy in copies:
        copy.start()
    for copy in copies[:2]:
        copy.wait()
    expert = lax.broadcasted_iota(jnp.int32, (n, rows), 0)
    gate = jnp.zeros((n, rows), jnp.float32)
    for k in range(choices):
        chosen = routes_buf[k : k + 1, :] == expert
        gate += jnp.where(chosen, weights_buf[k : k + 1, :], 0.0)
    gate = gate.T
    high = gate.astype(jnp.bfloat16).astype(jnp.float32)
    low = gate - high
    terms = []
    for r in range(0, rows, SUBLANES):
        terms += [high[r : r + SUBLANES], low[r : r + SUBLANES]]
    spare = width - len(terms) * n
    if spare:
        terms.append(jnp.zeros((SUBLANES, spare), jnp.float32))
    packed = jnp.concatenate(terms, axis=1).astype(jnp.bfloat16)
    for i in range(n):
        block_ref[i, rows:, :] = packed
    group = n // 8
    outs = []
    for i in range(8):
        part = pl.ds(i * group, group)
        for copy in copies[2 + i * group : 2 + (i + 1) * group]:
            copy.wait()
        outs.append(pltpu.make_async_copy(block_ref.at[part], send_ref.at[part], out_sem.at[i]))
        outs[-1].start()
    for out in outs:
        out.wait()


def pack(tokens, routes, route_weights, n, width):
    rows, choices = routes.shape
    shape = (n, rows + SUBLANES, width)
    operands = (tokens, routes.T, route_weights.T)
    return pl.pallas_call(
        pack_kernel,
        out_shape=pltpu.HBM(shape, jnp.bfloat16),
        in_specs=[HBM] * 3,
        out_specs=HBM,
        scratch_shapes=[
            pltpu.VMEM(shape, jnp.bfloat16),
            pltpu.VMEM((choices, rows), jnp.int32),
            pltpu.VMEM((choices, rows), jnp.float32),
            pltpu.SemaphoreType.DMA((n + 2,)),
            pltpu.SemaphoreType.DMA((8,)),
        ],
        compiler_params=params(8),
    )(*(pltpu.with_memory_space_constraint(operand, pltpu.HBM) for operand in operands))


def largest_kernel(weight_ref, held_ref, largest_ref, rest_ref, sem):
    experts = weight_ref.shape[0]
    kept = held_ref.shape[0]
    places = [held_ref.at[e] if e < kept else rest_ref.at[e - kept] for e in range(experts)]
    copies = [
        pltpu.make_async_copy(weight_ref.at[e], place, sem.at[e]) for e, place in enumerate(places)
    ]
    for copy in copies:
        copy.start()
    for e, copy in enumerate(copies):
        copy.wait()
        block = jnp.abs(places[e][...].astype(jnp.float32))
        row = jnp.max(block, axis=0, keepdims=True)
        top = jnp.max(row, axis=1, keepdims=True)
        largest_ref[e : e + 1, :] = jnp.broadcast_to(top, (1, LANES))


def hold(weights):
    experts, depth, ff = weights.shape
    kept = experts // 2
    return pl.pallas_call(
        largest_kernel,
        out_shape=(
            pltpu.VMEM((kept, depth, ff), weights.dtype),
            jax.ShapeDtypeStruct((experts, LANES), jnp.float32),
        ),
        in_specs=[HBM],
        out_specs=(VMEM, VMEM),
        scratch_shapes=[
            pltpu.VMEM((experts - kept, depth, ff), weights.dtype),
            pltpu.SemaphoreType.DMA((experts,)),
        ],
        compiler_params=params(12),
        cost_estimate=pl.CostEstimate(
            flops=2 * weights.size, bytes_accessed=2 * weights.size, transcendentals=0
        ),
    )(pltpu.with_memory_space_constraint(weights, pltpu.HBM))


def place(role, plane):
    index, core = lax.axis_index("expert"), lax.axis_index("tensor")
    beyond = jnp.bitwise_xor(lax.div(index, PLANE), plane)
    away = {0: 0, 1: 1 + core, 2: 2 - core, 3: 3}[role]
    return beyond * PLANE + jnp.bitwise_xor(lax.rem(index, PLANE), away)


def partial_kernel(*refs, rows, experts, roles):
    kept_ref, swapped_ref, tail_ref, held_ref, rest_ref, *refs = refs
    *out_refs, scaled_ref, total_ref = refs
    n, _, width = kept_ref.shape
    ff, depth, planes = held_ref.shape[1], 2 * width, n // PLANE
    chips = [[place(role, plane) for plane in range(planes)] for role in roles]
    left = lax.axis_index("tensor") == 0
    deep = experts // 2 * depth
    blocks = []
    for role, column in zip(roles, chips):
        row = lax.broadcasted_iota(jnp.int32, (SUBLANES, LANES), 0)
        top = jnp.zeros((SUBLANES, LANES), jnp.float32)
        for plane, chip in enumerate(column):
            value = jnp.broadcast_to(tail_ref[pl.ds(chip, 1), :], (SUBLANES, LANES))
            top = jnp.where(row == plane, value, top)
        blocks.append(out_refs.pop(0))
        if role in SENT:
            blocks[-1][blocks[-1].shape[0] - 1] = top.astype(jnp.bfloat16)
        else:
            out_refs.pop(0)[...] = top
    for i, chip in enumerate([chip for column in chips for chip in column]):
        at = flipped(chip, n)
        kept = kept_ref[at].astype(jnp.float32)
        swapped = swapped_ref[at, :rows].astype(jnp.float32)
        own = kept[:rows]
        x = jnp.concatenate([jnp.where(left, own, swapped), jnp.where(left, swapped, own)], axis=1)
        packed = kept[rows:]
        gates = jnp.concatenate(
            [
                packed[:, at : at + experts] + packed[:, at + experts : at + 2 * experts]
                for at in range(0, rows // SUBLANES * 2 * experts, 2 * experts)
            ],
            axis=0,
        )
        for e in range(experts):
            scaled_ref[i * rows : (i + 1) * rows, e * depth : (e + 1) * depth] = (
                x * gates[:, e : e + 1]
            ).astype(jnp.bfloat16)
    for i, part in enumerate((held_ref, rest_ref)):
        for at in range(0, ff, TILE):
            product = jnp.dot(
                scaled_ref[:, i * deep : (i + 1) * deep],
                part[:, at : at + TILE],
                preferred_element_type=jnp.float32,
            )
            if i == 0:
                total_ref[:, at : at + TILE] = product
                continue
            product += total_ref[:, at : at + TILE]
            for c, (role, block) in enumerate(zip(roles, blocks)):
                piece = product[c * planes * rows : (c + 1) * planes * rows]
                if role not in SENT:
                    block[:, at : at + TILE] = piece
                    continue
                for r in range(planes * rows // SUBLANES):
                    for lane in range(0, TILE, LANES):
                        block[r * (ff // LANES) + (at + lane) // LANES] = piece[
                            r * SUBLANES : (r + 1) * SUBLANES, lane : lane + LANES
                        ].astype(block.dtype)


def partials(got, tail, weights, rows, experts, roles):
    n, _, width = got[0].shape
    depth, planes = 2 * width, n // PLANE
    deep, ff = weights[0].shape
    count = planes * rows * len(roles)
    held, rest = (pltpu.with_memory_space_constraint(part, pltpu.VMEM) for part in weights)
    out_shape = ()
    for role in roles:
        if role in SENT:
            tiles = planes * rows * ff // (SUBLANES * LANES) + 1
            out_shape += (jax.ShapeDtypeStruct((tiles, SUBLANES, LANES), jnp.bfloat16),)
        else:
            out_shape += (
                jax.ShapeDtypeStruct((planes * rows, ff), jnp.float32),
                jax.ShapeDtypeStruct((SUBLANES, LANES), jnp.float32),
            )
    return pl.pallas_call(
        functools.partial(partial_kernel, rows=rows, experts=experts, roles=roles),
        out_shape=out_shape,
        in_specs=[VMEM] * 5,
        out_specs=(VMEM,) * len(out_shape),
        scratch_shapes=[
            pltpu.VMEM((count, experts * depth), jnp.bfloat16),
            pltpu.VMEM((count, ff), jnp.float32),
        ],
        compiler_params=params(16),
        cost_estimate=pl.CostEstimate(
            flops=2 * count * experts * depth * ff,
            bytes_accessed=4 * held.size,
            transcendentals=0,
        ),
    )(*got, tail, held, rest)


def finish_kernel(own_ref, largest_ref, *refs):
    plane_refs, (*crossed_refs, out_ref, top_ref) = refs[:2], refs[2:]
    rows, ff = out_ref.shape
    wide, tall = ff // LANES, rows // SUBLANES
    top = largest_ref[:1]
    tiles = [jnp.zeros((SUBLANES, LANES), jnp.float32)] * (wide * tall)
    for ref in (*plane_refs, *crossed_refs):
        tiles = [tile + ref[i].astype(jnp.float32) for i, tile in enumerate(tiles)]
        top = jnp.maximum(top, ref[ref.shape[0] - 1].astype(jnp.float32)[:1])
    total = [jnp.concatenate(tiles[i * wide : (i + 1) * wide], axis=1) for i in range(tall)]
    out_ref[...] = (own_ref[:rows] + jnp.concatenate(total)).astype(jnp.bfloat16)
    top_ref[0] = jnp.max(top)


def finish(own, largest, near, crossed, rows):
    operands = (own, largest, *near, *crossed)
    return pl.pallas_call(
        finish_kernel,
        out_shape=(
            jax.ShapeDtypeStruct((rows, own.shape[1]), jnp.bfloat16),
            jax.ShapeDtypeStruct((1,), jnp.float32),
        ),
        in_specs=[VMEM] * len(operands),
        out_specs=(VMEM, pl.BlockSpec(memory_space=pltpu.SMEM)),
        compiler_params=params(8),
    )(*operands)


def exchange(block):
    n = lax.axis_size("expert")
    order = [flipped(i, n) for i in range(n)]
    return lax.all_to_all(
        block, "expert", split_axis=0, concat_axis=0, tiled=True, axis_index_groups=[order]
    )


def over_tensor(largest):
    if lax.axis_size("tensor") == 2:
        return jnp.maximum(largest, lax.ppermute(largest, "tensor", [(0, 1), (1, 0)]))
    return lax.pmax(largest, "tensor")


def kernels(tokens, routes, route_weights, learner_weights):
    n = lax.axis_size("expert")
    rows = tokens.shape[0]
    experts, depth, ff = learner_weights.shape
    got = exchange(pack(tokens, routes, route_weights, n, depth // 2))
    held, largest = hold(learner_weights)
    largest = over_tensor(largest)
    weight = learner_weights.reshape(experts * depth, ff)
    held = held.reshape(-1, ff)
    got, held, largest, weight = lax.optimization_barrier((got, held, largest, weight))
    got = (got, lax.ppermute(got, "tensor", [(0, 1), (1, 0)]))
    rest = weight[held.shape[0] :]
    (across,) = partials(got, largest, (held, rest), rows, experts, (3,))
    second, second_largest, first = partials(got, largest, (held, rest), rows, experts, (2, 1))
    own, own_largest = partials(got, largest, (held, rest), rows, experts, (0,))

    def over_link(block, step):
        links = [(1 + core, 2 - core)[step] for core in range(2)]
        pairs = [(2 * i + c, 2 * (i ^ links[c]) + c) for i in range(n) for c in range(2)]
        return lax.ppermute(block, ("expert", "tensor"), pairs)

    def tiles_of(block):
        tiles = block.reshape(-1, SUBLANES, ff // LANES, LANES)
        return tiles.transpose(0, 2, 1, 3).reshape(-1, SUBLANES, LANES)

    across = over_link(across, 0).astype(jnp.float32)
    relay = jnp.concatenate(
        [across[:-1] + tiles_of(second), jnp.maximum(across[-1:], second_largest[None])]
    )
    near = [over_link(relay.astype(jnp.bfloat16), 1), over_link(first, 0)]
    planes = n // PLANE
    size = rows * ff // (SUBLANES * LANES)
    own_tiles = tiles_of(own)
    crossed = []
    for plane in sorted(range(1, planes), key=lambda plane: (plane != 2, plane)):
        total = own_tiles[plane * size : (plane + 1) * size]
        top = own_largest[plane]
        for block in near:
            total += block[plane * size : (plane + 1) * size].astype(jnp.float32)
            top = jnp.maximum(top, block[-1, plane].astype(jnp.float32))
        merged = jnp.concatenate([total, jnp.broadcast_to(top, (1, SUBLANES, LANES))])
        pairs = [(i, i ^ (plane * PLANE)) for i in range(n)]
        crossed.append(lax.ppermute(merged.astype(jnp.bfloat16), "expert", pairs))
    return finish(own, own_largest, near, crossed, rows)


def plain(tokens, routes, route_weights, learner_weights):
    n = lax.axis_size("expert")
    rows = tokens.shape[0]
    experts, depth, ff = learner_weights.shape
    largest = over_tensor(jnp.max(jnp.abs(learner_weights), axis=(1, 2)))
    chosen = routes[:, :, None] == jnp.arange(experts, dtype=jnp.int32)
    gate = jnp.sum(jnp.where(chosen, route_weights[:, :, None], 0.0), axis=1)
    high = lax.reduce_precision(gate, 8, 7)
    terms = jnp.concatenate([high, gate - high], axis=1).astype(jnp.bfloat16)
    columns = tokens.reshape(rows, n, depth).transpose(1, 0, 2)
    top = jnp.broadcast_to(largest[:, None, None], (n, rows, 1))
    got = jnp.concatenate([columns, jnp.broadcast_to(terms, (n, *terms.shape)), top], axis=2)
    got = lax.all_to_all(got, "expert", split_axis=0, concat_axis=0, tiled=True)
    weight = learner_weights.reshape(experts * depth, ff)

    def one(block):
        block = block.astype(jnp.float32)
        gates = block[:, depth : depth + experts] + block[:, depth + experts : depth + 2 * experts]
        scaled = (block[:, None, :depth] * gates[:, :, None]).astype(jnp.bfloat16)
        product = jnp.dot(
            scaled.reshape(rows, experts * depth), weight, preferred_element_type=jnp.float32
        )
        return product.astype(jnp.bfloat16)

    back = lax.map(one, got)
    back = lax.all_to_all(back, "expert", split_axis=0, concat_axis=0, tiled=True)
    combined = jnp.sum(back.astype(jnp.float32), axis=0).astype(jnp.bfloat16)
    expert_amax = jnp.max(got[:, 0, depth + 2 * experts]).astype(jnp.float32).reshape(1)
    return (combined, expert_amax)


def shards(tokens, routes, route_weights, learner_weights):
    n, rows = lax.axis_size("expert"), tokens.shape[0]
    experts, depth, ff = learner_weights.shape
    aligned = depth % (2 * LANES) == 0 and ff % TILE == 0 and rows % 32 == 0 and n in (8, 16, 32)
    fits = lax.axis_size("tensor") == 2 and rows // SUBLANES * 2 * experts <= depth // 2
    small = experts * depth * ff <= 4 << 20 and n * rows <= 1024 and n <= PLANE * SUBLANES
    form = kernels if aligned and fits and small and experts == n else plain
    return form(tokens, routes, route_weights, learner_weights)


def solution(mesh):
    return jax.shard_map(
        shards,
        mesh=mesh,
        in_specs=(
            P("expert", None),
            P("expert", None),
            P("expert", None),
            P(None, "expert", "tensor"),
        ),
        out_specs=(P("expert", "tensor"), P("expert")),
        check_vma=False,
    )
```
